32 devices in a mesh: panel: 4 (over x, core), obs: 8 (over z, y).
Axes of the slice: x: 2, y: 2, z: 4, core: 2. Of those that a mesh axis runs over, the one named last changes fastest.
Arguments:
- les_rows: bfloat16 [4096, 2, 128], P(('panel', 'obs')), may hold values from -6 to 6
- les_dest: int32 [4096, 1], P(('panel', 'obs')), may hold values from 0 to 31; in each aligned block of 128 rows (0 to 127, 128 to 255, ...) at most 8 rows name the same one
- loading_weight: bfloat16 [8192, 1024], P('panel', 'obs'), may hold values from -0.09375 to 0.09375
- thickness_weight: bfloat16 [8192, 1024], P('panel', 'obs'), may hold values from -0.09375 to 0.09375
- delays: int32 [16, 8], P('panel', 'obs'), may hold values from 0 to 64
Outputs:
- acoustic_pressure: float32 [128, 1024], P('panel', 'obs')
The draws below stay inside these ranges and needn't reach their ends.
Inputs may be any that keep to these rules, and one draw needn't show every extreme that they name: `les_dest`: in the aligned blocks of 128 rows of one LES owner, no destination is named by more than 8 rows, a bound that some block reaches; every destination is named by some row.
All inputs are finite; a program needn't handle non-finite values.
Results may differ from the reference program's by a relative error of at most 0.0018.
Values may be sent and summed in bfloat16 or wider, within the bound.
No kernel may reach another device: no remote copies, remote signals or barrier semaphores. Data moves between devices by JAX's collectives and lax.ppermute only.
A program may use at most 64 MiB of HBM per device.

```python
import math
import jax
import jax.numpy as jnp
import numpy as np
from jax import lax

TS = 128
ROWS_DEV = 128
PBLK = 512
OBLK = 128
DMAX = 64
CAP = 8
SLOTS_DEV = 256
PANELS = 8192
ROWS_TOTAL = 4096
OBSERVERS = 1024
N_PANEL = 4
N_OBS = 8
DEVICES = 32


def place_ends(drawn, key, low, high):
    spot = [jax.random.randint(jax.random.fold_in(key, axis), (), 0, length) for axis, length in enumerate(drawn.shape)]
    longest = drawn.shape.index(max(drawn.shape))
    next_to = spot[:longest] + [(spot[longest] + 1) % drawn.shape[longest]] + spot[longest + 1:]
    return drawn.at[tuple(spot)].set(low).at[tuple(next_to)].set(high)


def steps_of(stream_key, shape, cuts, least, largest):
    level = 1.0
    for position, shards_of in cuts:
        steps = jax.random.uniform(jax.random.fold_in(jax.random.fold_in(stream_key, 6), position), (shards_of,), jnp.float32, least / len(cuts), largest / len(cuts))
        level = level * jnp.repeat(jnp.exp(steps), shape[position] // shards_of).reshape((-1,) + (1,) * (len(shape) - 1 - position))
    return level


def deal_out(key, own, number, rows, number_of, top, reach, lean):
    ranking = jax.random.permutation(key, number_of)
    heavy_load, ordinary = load_shares(number_of, rows * top, reach, lean, True), load_shares(number_of, rows * top, reach, lean, False)
    places = jnp.arange(number_of)

    def named(tallies, rotation):
        used = int((tallies > 0).sum())
        fixed = max(1, used // 4)
        shifted = fixed + (places - fixed + rotation * (used - fixed)) % max(1, number_of - fixed)
        return jnp.zeros((number_of,), jnp.int32).at[ranking[jnp.where(places < fixed, places, shifted)]].set(jnp.asarray(tallies, jnp.int32))

    tallies = jnp.where(number % 4 == 0, named(heavy_load, number // 4), named(ordinary, number - number // 4 - 1))
    mixed = jax.random.permutation(jax.random.fold_in(own, 3), number_of)
    donor, receiver = mixed[0:number_of // 2 * 2:2], mixed[1:number_of // 2 * 2:2]
    room = jnp.minimum(tallies[donor] - 1, reach - tallies[receiver]) // 2
    room = jnp.where((donor == ranking[0]) | (receiver == ranking[0]) | (tallies[receiver] == 0), 0, jnp.maximum(room, 0))
    shifted = jax.random.randint(jax.random.fold_in(own, 4), (number_of // 2,), 0, 1 << 20) % (room + 1)
    tallies = tallies.at[donor].add(-shifted).at[receiver].add(shifted)
    members = jnp.searchsorted(jnp.cumsum(tallies), jnp.arange(rows * top), side="right").astype(jnp.int32)
    table = members.reshape(top, rows).T
    table = table[jax.random.permutation(jax.random.fold_in(own, 1), rows)]
    rotation = jax.random.randint(jax.random.fold_in(own, 2), (rows, 1), 0, top)
    return jnp.take_along_axis(table, (jnp.arange(top)[None, :] + rotation) % top, axis=1)


def load_shares(amount, total, limit, skew, full):
    portions = [(1 << 20) // math.isqrt(standing ** skew) + 1 for standing in range(1, amount + 1)]
    largest = limit if full else min(limit, max(-(-total // amount), total * portions[0] // sum(portions)))
    least = 1 if total - largest >= amount - 1 else 0
    holding, rest = [largest] + [least] * (amount - 1), total - largest - least * (amount - 1)
    while rest > 0:
        candidates = [i for i in range(1, amount) if holding[i] < largest] or [i for i in range(1, amount) if holding[i] < limit]
        mass, left = sum([portions[i] for i in candidates]), rest
        for i in candidates:
            addition = min(limit - holding[i], max(1, left * portions[i] // mass), rest)
            holding[i] = holding[i] + addition
            rest = rest - addition
    return np.array(holding)


def centred(own_key, shape, scale, bound, split=(), kind=jnp.bfloat16):
    drawn = jax.random.normal(own_key, shape, jnp.float32) * scale
    if len(split) > 0:
        drawn = steps_of(own_key, shape, split, -0.22, 0.18) * drawn
    return jnp.clip(drawn, min=-bound, max=bound).astype(kind)


def setup_inputs(seed: int = 0) -> dict:
    seeds = jax.random.split(jax.random.key(seed), 6)
    les_rows = centred(seeds[0], (ROWS_TOTAL, 2, TS), 1.0, 6.0, ((0, 32),))
    les_dest_keys = jax.random.split(jax.random.fold_in(seeds[1], 1), ROWS_TOTAL // ROWS_DEV)
    les_dest_turns = jax.random.permutation(jax.random.fold_in(seeds[1], 3), ROWS_TOTAL // ROWS_DEV)
    les_dest = jax.vmap(lambda own, number: deal_out(jax.random.fold_in(seeds[1], 2), own, number, ROWS_DEV, DEVICES, 1, CAP, 2))(les_dest_keys, les_dest_turns).reshape((ROWS_TOTAL, 1))
    loading_weight = centred(seeds[2], (PANELS, OBSERVERS), (PANELS // 2) ** -0.5, 0.09375, ((0, 4), (1, 8)))
    thickness_weight = centred(seeds[3], (PANELS, OBSERVERS), (PANELS // 2) ** -0.5, 0.09375, ((0, 4), (1, 8)))
    delays = place_ends(jax.random.randint(seeds[4], (PANELS // PBLK, OBSERVERS // OBLK), 0, DMAX + 1), jax.random.fold_in(seeds[4], 1), 0, DMAX).astype(jnp.int32)
    return dict(les_rows=les_rows, les_dest=les_dest, loading_weight=loading_weight, thickness_weight=thickness_weight, delays=delays)


def owner_ranks(dest_block, count):
    onehot = (dest_block[:, :, None] == jnp.arange(count, dtype=jnp.int32)[None, None, :]).astype(jnp.int32)
    earlier = jnp.cumsum(onehot, axis=1) - onehot
    return jnp.sum(earlier * onehot, axis=2).astype(jnp.int32)


def delay_block(block, delay):
    steps = block.shape[0]
    padded = jnp.concatenate([jnp.zeros_like(block), block], axis=0)
    start = (steps - delay).astype(jnp.int32)
    return lax.dynamic_slice_in_dim(padded, start, steps, 0)


def shift_time(values, delay_row):
    steps = values.shape[0]
    blocks = delay_row.shape[0]
    shaped = values.reshape(steps, blocks, -1)
    moved = jax.vmap(delay_block, in_axes=(1, 0), out_axes=1)(shaped, delay_row.astype(jnp.int32))
    return moved.reshape(steps, -1)


def reference(les_rows, les_dest, loading_weight, thickness_weight, delays):
    count = N_PANEL * N_OBS
    dest_block = les_dest[:, 0].astype(jnp.int32).reshape(count, ROWS_DEV)
    rank = owner_ranks(dest_block, count)
    owner = jnp.arange(count, dtype=jnp.int32)[:, None]
    slot = (dest_block * SLOTS_DEV + owner * CAP + rank).reshape(-1)
    surface = jnp.zeros((PANELS, 2, TS), les_rows.dtype).at[slot].set(les_rows)
    velocity = surface[:, 1, :].astype(jnp.float32)
    padded = jnp.pad(velocity, ((0, 0), (1, 1)))
    rate = ((padded[:, 2:] - padded[:, :-2]) * 0.5).astype(jnp.bfloat16)
    pressure_src = surface[:, 0, :]
    nblocks = PANELS // PBLK
    press_blocks = pressure_src.reshape(nblocks, PBLK, TS)
    rate_blocks = rate.reshape(nblocks, PBLK, TS)
    load_blocks = loading_weight.reshape(nblocks, PBLK, OBSERVERS)
    thick_blocks = thickness_weight.reshape(nblocks, PBLK, OBSERVERS)

    def one_block(total, inputs):
        press_b, rate_b, load_b, thick_b, delay_b = inputs
        dims = (((0,), (0,)), ((), ()))
        term = lax.dot_general(press_b, load_b, dims, preferred_element_type=jnp.float32)
        term = term + lax.dot_general(rate_b, thick_b, dims, preferred_element_type=jnp.float32)
        return total + shift_time(term, delay_b), None

    start = jnp.zeros((TS, OBSERVERS), jnp.float32)
    total, unused = lax.scan(one_block, start, (press_blocks, rate_blocks, load_blocks, thick_blocks, delays))
    return total
```

```python
import functools

import jax
import jax.numpy as jnp
from jax import lax
from jax.experimental import pallas as pl
from jax.experimental.pallas import tpu as pltpu
from jax.sharding import PartitionSpec as P

PBLK = 512
EXTRA = 16
VMEM_LIMIT = 48 * 1024 * 1024


def dot(a, b):
    return lax.dot_general(a, b, (((1,), (0,)), ((), ())), preferred_element_type=jnp.float32)


def slot_kernel(n_panel, n_obs, cap, a_ref, b_ref, ya_ref, yb_ref, out_ref, slots_ref):
    count = n_panel * n_obs
    me_p = lax.axis_index("panel")
    me_o = lax.axis_index("obs")
    rows = a_ref.shape[0] // (n_obs // 4) - EXTRA
    steps = a_ref.shape[1] // 2
    per = 16 // cap
    half = n_obs // 4
    r0 = lax.broadcasted_iota(jnp.int32, (rows, rows), 0)
    r1 = lax.broadcasted_iota(jnp.int32, (rows, rows), 1)
    earlier = (r0 < r1).astype(jnp.bfloat16)
    t0 = lax.broadcasted_iota(jnp.int32, (steps, steps), 0)
    t1 = lax.broadcasted_iota(jnp.int32, (steps, steps), 1)
    slope = jnp.where(t0 == t1 + 1, 0.5, jnp.where(t0 == t1 - 1, -0.5, 0.0)).astype(jnp.bfloat16)
    dest_ids = lax.broadcasted_iota(jnp.int32, (count, rows), 0)
    slot_ids = lax.broadcasted_iota(jnp.int32, (count * 16, per * rows), 0)
    for quad in range(n_obs // per):
        values, places = [], []
        for i in range(per):
            j = quad * per + i
            k, y = j // 2, j % 2
            ref = ((a_ref, ya_ref), (b_ref, yb_ref))[k // half][y]
            base = (k % half) * (rows + EXTRA)
            dest = ref[base + rows : base + rows + EXTRA, 0:rows].astype(jnp.float32)[0:1]
            dest = dest.astype(jnp.int32)
            onehot = dest_ids == dest
            before = dot(onehot.astype(jnp.bfloat16), earlier)
            rank = jnp.sum(jnp.where(onehot, before, 0.0), axis=0, keepdims=True).astype(jnp.int32)
            within = ((me_o % per) ^ i) * cap + rank
            places.append((dest ^ (me_p * n_obs)) * 16 + within)
            rate = dot(ref[base : base + rows, steps:], slope).astype(jnp.bfloat16)
            values.append(jnp.concatenate([ref[base : base + rows, 0:steps], rate], axis=1))
        value = jnp.concatenate(values, axis=0)
        place = jnp.concatenate(places, axis=1)
        pick = (slot_ids == place).astype(jnp.bfloat16)
        got = dot(pick, value).astype(jnp.bfloat16)
        start = pl.multiple_of(((me_o // per) ^ quad) * 16, 16)
        slots_ref[:, pl.ds(start, 16), :] = got.reshape(count, 16, 2 * steps)
    for k in range(out_ref.shape[0]):
        block = slots_ref[2 * k : 2 * k + 2].reshape(2 * n_obs * cap, 2 * steps)
        out_ref[k, :, 0 : 2 * n_obs * cap] = block[:, 0:steps].T
        out_ref[k, :, 2 * n_obs * cap :] = block[:, steps:].T


def add_term(acc_ref, source, weights, delay):
    steps = source.shape[0]
    acc_ref[pl.ds(delay, steps), :] += dot(source, weights)


def near_kernel(n_obs, s_ref, load_ref, thick_ref, delay_ref, c_ref, out_ref, acc_ref):
    me_p = lax.axis_index("panel")
    steps = out_ref.shape[0]
    nblocks = n_obs // 2
    acc_ref[...] = jnp.zeros_like(acc_ref)
    width = load_ref.shape[2]
    for b in range(nblocks):
        weights = jnp.concatenate(
            [ref[2 * b + i, me_p] for ref in (load_ref, thick_ref) for i in range(2)], axis=0
        )
        add_term(acc_ref, s_ref[b], weights, delay_ref[b, 0])
    piece_terms(nblocks, width, s_ref, nblocks, c_ref, acc_ref)
    out_ref[...] = acc_ref[0:steps]


def piece_terms(nblocks, width, s_ref, first, w_ref, acc_ref):
    depth = 2 * width * nblocks
    delays = w_ref[2 * depth : 2 * depth + EXTRA, :].astype(jnp.float32)[0:1].astype(jnp.int32)
    for b in range(nblocks):
        lo, hi = 2 * width * b, 2 * width * (b + 1)
        weights = jnp.concatenate([w_ref[lo:hi], w_ref[depth + lo : depth + hi]], axis=0)
        add_term(acc_ref, s_ref[first + b], weights, delays[0, b])


def far_kernel(n_panel, n_obs, width, s_ref, near_ref, x_ref, xc_ref, *refs):
    outs, acc_ref = refs[:n_panel], refs[n_panel]
    me_p = lax.axis_index("panel")
    steps = near_ref.shape[0]
    nblocks = n_obs // 2
    acc_ref[0:steps] = near_ref[...]
    acc_ref[steps:] = jnp.zeros_like(acc_ref[steps:])
    piece_terms(nblocks, width, s_ref, 2 * nblocks, x_ref, acc_ref)
    piece_terms(nblocks, width, s_ref, 3 * nblocks, xc_ref, acc_ref)
    share = steps // n_panel
    for k in range(n_panel):
        start = pl.multiple_of((me_p ^ k) * share, share)
        outs[k][...] = acc_ref[pl.ds(start, share), :]


def per_device(les_rows, les_dest, loading_weight, thickness_weight, delays):
    n_panel = lax.axis_size("panel")
    n_obs = lax.axis_size("obs")
    count = n_panel * n_obs
    rows, _, steps = les_rows.shape
    cap = 2 * rows // count
    observers = loading_weight.shape[1]
    width = n_obs * cap
    nblocks = n_obs // 2
    me_p = lax.axis_index("panel")
    params = pltpu.CompilerParams(vmem_limit_bytes=VMEM_LIMIT)
    vmem = pl.BlockSpec(memory_space=pltpu.VMEM)
    smem = pl.BlockSpec(memory_space=pltpu.SMEM)

    def along_panel(value, k):
        return lax.ppermute(value, "panel", [(i, i ^ k) for i in range(n_panel)])

    def along_obs(value, k):
        return lax.ppermute(value, "obs", [(i, i ^ k) for i in range(n_obs)])

    load = loading_weight.reshape(n_obs, n_panel, width, observers)
    thick = thickness_weight.reshape(n_obs, n_panel, width, observers)
    delay_rows = jnp.pad(
        delays.reshape(1, nblocks).astype(jnp.bfloat16),
        ((0, EXTRA - 1), (0, observers - nblocks)),
    )

    def piece(k):
        parts = [
            lax.dynamic_index_in_dim(w, me_p ^ k, 1, False).reshape(n_obs * width, observers)
            for w in (load, thick)
        ]
        return along_panel(jnp.concatenate(parts + [delay_rows], axis=0), k)

    from_x, from_xc, from_c = piece(2), piece(3), piece(1)

    dest_rows = jnp.pad(
        les_dest.reshape(1, rows).astype(jnp.bfloat16), ((0, EXTRA - 1), (0, 2 * steps - rows))
    )
    message = jnp.concatenate([les_rows.reshape(rows, 2 * steps), dest_rows], axis=0)
    column = [message] + [along_obs(message, 2 * k) for k in range(1, n_obs // 2)]
    a = jnp.concatenate(column[: n_obs // 4], axis=0)
    b = jnp.concatenate(column[n_obs // 4 :], axis=0)
    ya, yb = along_obs(a, 1), along_obs(b, 1)

    sources = pl.pallas_call(
        functools.partial(slot_kernel, n_panel, n_obs, cap),
        out_shape=jax.ShapeDtypeStruct((count // 2, steps, 4 * width), jnp.bfloat16),
        in_specs=[vmem] * 4,
        out_specs=vmem,
        scratch_shapes=[pltpu.VMEM((count, width, 2 * steps), jnp.bfloat16)],
        compiler_params=params,
    )(a, b, ya, yb)
    acc = pltpu.VMEM((2 * steps, observers), jnp.float32)
    near = pl.pallas_call(
        functools.partial(near_kernel, n_obs),
        out_shape=jax.ShapeDtypeStruct((steps, observers), jnp.float32),
        in_specs=[vmem, vmem, vmem, smem, vmem],
        out_specs=vmem,
        scratch_shapes=[acc],
        compiler_params=params,
    )(sources, load, thick, delays, from_c)
    share = jax.ShapeDtypeStruct((steps // n_panel, observers), jnp.float32)
    shares = pl.pallas_call(
        functools.partial(far_kernel, n_panel, n_obs, width),
        out_shape=[share] * n_panel,
        in_specs=[vmem] * 4,
        out_specs=[vmem] * n_panel,
        scratch_shapes=[acc],
        compiler_params=params,
    )(sources, near, from_x, from_xc)
    total = shares[0]
    for k in (2, 3, 1):
        total = total + along_panel(shares[k], k)
    return total


def solution(mesh):
    placed = (
        P(("panel", "obs"), None, None),
        P(("panel", "obs"), None),
        P("panel", "obs"),
        P("panel", "obs"),
        P("panel", "obs"),
    )
    return jax.shard_map(
        per_device, mesh=mesh, in_specs=placed, out_specs=P("panel", "obs"), check_vma=False
    )
```

```python
import functools

import jax
import jax.numpy as jnp
from jax import lax
from jax.experimental import pallas as pl
from jax.experimental.pallas import tpu as pltpu
from jax.sharding import PartitionSpec as P

PBLK = 512
PACK_ORDER = (2, 3, 1, 0)
EXTRA = 16
VMEM_LIMIT = 48 * 1024 * 1024


def dot(a, b):
    return lax.dot_general(a, b, (((1,), (0,)), ((), ())), preferred_element_type=jnp.float32)


def pack_kernel(n_panel, n_obs, cap, rows_ref, dest_ref, delay_ref, load_ref, thick_ref, *refs):
    message_ref, pieces = refs[0], refs[1 : 1 + n_panel]
    rows_in, dest_in, delay_in, sems, few = refs[1 + n_panel :]
    count = n_panel * n_obs
    me_p = lax.axis_index("panel")
    width = n_obs * cap
    depth = n_obs * width
    small = [
        pltpu.make_async_copy(src, dst, few.at[i])
        for i, (src, dst) in enumerate(((rows_ref, rows_in), (dest_ref, dest_in), (delay_ref, delay_in)))
    ]
    for copy in small:
        copy.start()
    copies = []
    for k in PACK_ORDER:
        for i, ref in enumerate((load_ref, thick_ref)):
            there = pieces[k].at[pl.ds(i * depth, depth)].reshape(n_obs, width, ref.shape[3])
            copies.append(pltpu.make_async_copy(ref.at[:, me_p ^ k], there, sems.at[k, i]))
            copies[-1].start()
    rows, steps = rows_ref.shape[0] // 2, rows_ref.shape[1]
    nblocks = delay_ref.shape[1]
    for copy in small:
        copy.wait()
    lane = lax.broadcasted_iota(jnp.int32, (EXTRA, load_ref.shape[3]), 1)
    late = jnp.zeros(lane.shape, jnp.int32)
    for b in range(nblocks):
        late = jnp.where(lane == b, delay_in[0, b], late)
    for k in range(n_panel):
        pieces[k][2 * depth : 2 * depth + EXTRA, :] = late.astype(jnp.float32).astype(jnp.bfloat16)
    r0 = lax.broadcasted_iota(jnp.int32, (rows, 2 * rows), 0)
    r1 = lax.broadcasted_iota(jnp.int32, (rows, 2 * rows), 1)
    value = rows_in[...]
    pressure = dot((r1 == 2 * r0).astype(jnp.bfloat16), value).astype(jnp.bfloat16)
    velocity = dot((r1 == 2 * r0 + 1).astype(jnp.bfloat16), value).astype(jnp.bfloat16)
    t0 = lax.broadcasted_iota(jnp.int32, (steps, steps), 0)
    t1 = lax.broadcasted_iota(jnp.int32, (steps, steps), 1)
    slope = jnp.where(t0 == t1 + 1, 0.5, jnp.where(t0 == t1 - 1, -0.5, 0.0)).astype(jnp.bfloat16)
    message_ref[0:rows, 0:steps] = pressure
    message_ref[0:rows, steps:] = dot(velocity, slope).astype(jnp.bfloat16)
    dest = dest_in[...]
    onehot = lax.broadcasted_iota(jnp.int32, (count, rows), 0) == dest
    q0 = lax.broadcasted_iota(jnp.int32, (rows, rows), 0)
    q1 = lax.broadcasted_iota(jnp.int32, (rows, rows), 1)
    before = dot(onehot.astype(jnp.bfloat16), (q0 < q1).astype(jnp.bfloat16))
    rank = jnp.sum(jnp.where(onehot, before, 0.0), axis=0, keepdims=True)
    tail = jnp.zeros((EXTRA, steps), jnp.float32)
    message_ref[rows:, 0:steps] = (tail + dest.astype(jnp.float32)).astype(jnp.bfloat16)
    message_ref[rows:, steps:] = (tail + rank).astype(jnp.bfloat16)
    for copy in copies:
        copy.wait()


def slot_kernel(n_panel, n_obs, cap, a_ref, b_ref, ya_ref, yb_ref, gate_ref, out_ref, slots_ref):
    count = n_panel * n_obs
    me_p = lax.axis_index("panel")
    me_o = lax.axis_index("obs")
    rows = a_ref.shape[0] // (n_obs // 4) - EXTRA
    steps = a_ref.shape[1] // 2
    per = 16 // cap
    slot_ids = lax.broadcasted_iota(jnp.int32, (count * 16, per * rows), 0)
    for quad in range(n_obs // per):
        values, places = [], []
        for i in range(per):
            j = quad * per + i
            ref = (a_ref, ya_ref, b_ref, yb_ref)[j % 4]
            base = (j // 4) * (rows + EXTRA)
            tail = ref[base + rows : base + rows + EXTRA, :].astype(jnp.float32)[0:1].astype(jnp.int32)
            dest, rank = tail[:, 0:rows], tail[:, steps : steps + rows]
            within = ((me_o % per) ^ i) * cap + rank
            places.append((dest ^ (me_p * n_obs)) * 16 + within)
            values.append(ref[base : base + rows, :])
        value = jnp.concatenate(values, axis=0)
        place = jnp.concatenate(places, axis=1)
        pick = (slot_ids == place).astype(jnp.bfloat16)
        got = dot(pick, value).astype(jnp.bfloat16)
        start = pl.multiple_of(((me_o // per) ^ quad) * 16, 16)
        slots_ref[:, pl.ds(start, 16), :] = got.reshape(count, 16, 2 * steps)
    for k in range(out_ref.shape[0]):
        block = slots_ref[2 * k : 2 * k + 2].reshape(2 * n_obs * cap, 2 * steps)
        out_ref[k, :, 0 : 2 * n_obs * cap] = block[:, 0:steps].T
        out_ref[k, :, 2 * n_obs * cap :] = block[:, steps:].T


def add_term(acc_ref, source, weights, delay):
    steps = source.shape[0]
    acc_ref[pl.ds(delay, steps), :] += dot(source, weights)


def late_kernel(depth, x_ref, xc_ref, out_ref):
    for i, ref in enumerate((x_ref, xc_ref)):
        out_ref[8 * i : 8 * i + 8] = ref[depth : depth + EXTRA, :].astype(jnp.float32)[0:8].astype(jnp.int32)


def near_kernel(n_obs, width, s_ref, own_ref, c_ref, out_ref, acc_ref):
    steps = out_ref.shape[0]
    nblocks = n_obs // 2
    acc_ref[...] = jnp.zeros_like(acc_ref)
    piece_terms(nblocks, width, s_ref, 0, own_ref, acc_ref)
    piece_terms(nblocks, width, s_ref, nblocks, c_ref, acc_ref)
    out_ref[...] = acc_ref[0:steps]


def piece_terms(nblocks, width, s_ref, first, w_ref, acc_ref):
    depth = 2 * width * nblocks
    delays = w_ref[2 * depth : 2 * depth + EXTRA, :].astype(jnp.float32)[0:1].astype(jnp.int32)
    for b in range(nblocks):
        lo, hi = 2 * width * b, 2 * width * (b + 1)
        weights = jnp.concatenate([w_ref[lo:hi], w_ref[depth + lo : depth + hi]], axis=0)
        add_term(acc_ref, s_ref[first + b], weights, delays[0, b])


def far_kernel(n_panel, n_obs, width, s_ref, near_ref, x_ref, xc_ref, *refs):
    outs, acc_ref = refs[:n_panel], refs[n_panel]
    me_p = lax.axis_index("panel")
    steps = near_ref.shape[0]
    nblocks = n_obs // 2
    acc_ref[0:steps] = near_ref[...]
    acc_ref[steps:] = jnp.zeros_like(acc_ref[steps:])
    piece_terms(nblocks, width, s_ref, 2 * nblocks, x_ref, acc_ref)
    piece_terms(nblocks, width, s_ref, 3 * nblocks, xc_ref, acc_ref)
    share = steps // n_panel
    for k in range(n_panel):
        start = pl.multiple_of((me_p ^ k) * share, share)
        outs[k][...] = acc_ref[pl.ds(start, share), :]


def per_device(les_rows, les_dest, loading_weight, thickness_weight, delays):
    n_panel = lax.axis_size("panel")
    n_obs = lax.axis_size("obs")
    count = n_panel * n_obs
    rows, _, steps = les_rows.shape
    cap = 2 * rows // count
    observers = loading_weight.shape[1]
    width = n_obs * cap
    nblocks = n_obs // 2
    params = pltpu.CompilerParams(vmem_limit_bytes=VMEM_LIMIT)
    vmem = pl.BlockSpec(memory_space=pltpu.VMEM)
    hbm = pl.BlockSpec(memory_space=pltpu.HBM)

    def along_panel(value, k):
        return lax.ppermute(value, "panel", [(i, i ^ k) for i in range(n_panel)])

    def along_obs(value, k):
        return lax.ppermute(value, "obs", [(i, i ^ k) for i in range(n_obs)])

    load = loading_weight.reshape(n_obs, n_panel, width, observers)
    thick = thickness_weight.reshape(n_obs, n_panel, width, observers)
    piece = jax.ShapeDtypeStruct((2 * n_obs * width + EXTRA, observers), jnp.bfloat16)
    message, own, to_c, to_x, to_xc = pl.pallas_call(
        functools.partial(pack_kernel, n_panel, n_obs, cap),
        out_shape=[jax.ShapeDtypeStruct((rows + EXTRA, 2 * steps), jnp.bfloat16)] + [piece] * n_panel,
        in_specs=[hbm] * 5,
        out_specs=[vmem] * (1 + n_panel),
        scratch_shapes=[
            pltpu.VMEM((2 * rows, steps), jnp.bfloat16),
            pltpu.VMEM((1, rows), jnp.int32),
            pltpu.SMEM((1, nblocks), jnp.int32),
            pltpu.SemaphoreType.DMA((n_panel, 2)),
            pltpu.SemaphoreType.DMA((3,)),
        ],
        compiler_params=params,
    )(
        *(
            pltpu.with_memory_space_constraint(value, pltpu.HBM)
            for value in (
                les_rows.reshape(2 * rows, steps),
                les_dest.reshape(1, rows),
                delays.reshape(1, nblocks),
                load,
                thick,
            )
        )
    )
    from_x, from_xc, from_c = along_panel(to_x, 2), along_panel(to_xc, 3), along_panel(to_c, 1)
    a = jnp.concatenate([message] + [along_obs(message, k) for k in range(4, n_obs, 4)], axis=0)
    a, from_c = lax.optimization_barrier((a, from_c))
    b, ya, yb = along_obs(a, 2), along_obs(a, 1), along_obs(a, 3)

    late = pl.pallas_call(
        functools.partial(late_kernel, 2 * n_obs * width),
        out_shape=jax.ShapeDtypeStruct((16, observers), jnp.int32),
        in_specs=[vmem] * 2,
        out_specs=vmem,
        compiler_params=params,
        cost_estimate=pl.CostEstimate(flops=10**0, bytes_accessed=0, transcendentals=0),
    )(from_x, from_xc)

    sources = pl.pallas_call(
        functools.partial(slot_kernel, n_panel, n_obs, cap),
        out_shape=jax.ShapeDtypeStruct((count // 2, steps, 4 * width), jnp.bfloat16),
        in_specs=[vmem] * 5,
        out_specs=vmem,
        scratch_shapes=[pltpu.VMEM((count, width, 2 * steps), jnp.bfloat16)],
        compiler_params=params,
    )(a, b, ya, yb, late)
    acc = pltpu.VMEM((2 * steps, observers), jnp.float32)
    near = pl.pallas_call(
        functools.partial(near_kernel, n_obs, width),
        out_shape=jax.ShapeDtypeStruct((steps, observers), jnp.float32),
        in_specs=[vmem] * 3,
        out_specs=vmem,
        scratch_shapes=[acc],
        compiler_params=params,
    )(sources, own, from_c)
    share = jax.ShapeDtypeStruct((steps // n_panel, observers), jnp.float32)
    shares = pl.pallas_call(
        functools.partial(far_kernel, n_panel, n_obs, width),
        out_shape=[share] * n_panel,
        in_specs=[vmem] * 4,
        out_specs=[vmem] * n_panel,
        scratch_shapes=[acc],
        compiler_params=params,
    )(sources, near, from_x, from_xc)
    total = shares[0]
    for k in (2, 3, 1):
        total = total + along_panel(shares[k], k)
    return total


def solution(mesh):
    placed = (
        P(("panel", "obs"), None, None),
        P(("panel", "obs"), None),
        P("panel", "obs"),
        P("panel", "obs"),
        P("panel", "obs"),
    )
    return jax.shard_map(
        per_device, mesh=mesh, in_specs=placed, out_specs=P("panel", "obs"), check_vma=False
    )
```

```python
import functools

import jax
import jax.numpy as jnp
from jax import lax
from jax.experimental import pallas as pl
from jax.experimental.pallas import tpu as pltpu
from jax.sharding import PartitionSpec as P

PBLK = 512
PACK_ORDER = (2, 3, 1, 0)
EXTRA = 16
VMEM_LIMIT = 48 * 1024 * 1024


def dot(a, b):
    return lax.dot_general(a, b, (((1,), (0,)), ((), ())), preferred_element_type=jnp.float32)


def pack_kernel(n_panel, n_obs, cap, rows_ref, dest_ref, delay_ref, load_ref, thick_ref, *refs):
    message_ref, pieces = refs[0], refs[1 : 1 + n_panel]
    rows_in, dest_in, delay_in, sems, few = refs[1 + n_panel :]
    count = n_panel * n_obs
    me_p = lax.axis_index("panel")
    width = n_obs * cap
    depth = n_obs * width
    small = [
        pltpu.make_async_copy(src, dst, few.at[i])
        for i, (src, dst) in enumerate(((rows_ref, rows_in), (dest_ref, dest_in), (delay_ref, delay_in)))
    ]
    for copy in small:
        copy.start()
    copies = []
    for k in PACK_ORDER:
        for i, ref in enumerate((load_ref, thick_ref)):
            there = pieces[k].at[pl.ds(i * depth, depth)].reshape(n_obs, width, ref.shape[3])
            copies.append(pltpu.make_async_copy(ref.at[:, me_p ^ k], there, sems.at[k, i]))
            copies[-1].start()
    rows, steps = rows_ref.shape[0] // 2, rows_ref.shape[1]
    nblocks = delay_ref.shape[1]
    for copy in small:
        copy.wait()
    lane = lax.broadcasted_iota(jnp.int32, (EXTRA, load_ref.shape[3]), 1)
    late = jnp.zeros(lane.shape, jnp.int32)
    for b in range(nblocks):
        late = jnp.where(lane == b, delay_in[0, b], late)
    for k in range(n_panel):
        pieces[k][2 * depth : 2 * depth + EXTRA, :] = late.astype(jnp.float32).astype(jnp.bfloat16)
    r0 = lax.broadcasted_iota(jnp.int32, (rows, 2 * rows), 0)
    r1 = lax.broadcasted_iota(jnp.int32, (rows, 2 * rows), 1)
    value = rows_in[...]
    pressure = dot((r1 == 2 * r0).astype(jnp.bfloat16), value).astype(jnp.bfloat16)
    velocity = dot((r1 == 2 * r0 + 1).astype(jnp.bfloat16), value).astype(jnp.bfloat16)
    t0 = lax.broadcasted_iota(jnp.int32, (steps, steps), 0)
    t1 = lax.broadcasted_iota(jnp.int32, (steps, steps), 1)
    slope = jnp.where(t0 == t1 + 1, 0.5, jnp.where(t0 == t1 - 1, -0.5, 0.0)).astype(jnp.bfloat16)
    message_ref[0:rows, 0:steps] = pressure
    message_ref[0:rows, steps:] = dot(velocity, slope).astype(jnp.bfloat16)
    dest = dest_in[...]
    onehot = lax.broadcasted_iota(jnp.int32, (count, rows), 0) == dest
    q0 = lax.broadcasted_iota(jnp.int32, (rows, rows), 0)
    q1 = lax.broadcasted_iota(jnp.int32, (rows, rows), 1)
    before = dot(onehot.astype(jnp.bfloat16), (q0 < q1).astype(jnp.bfloat16))
    rank = jnp.sum(jnp.where(onehot, before, 0.0), axis=0, keepdims=True)
    tail = jnp.zeros((EXTRA, steps), jnp.float32)
    message_ref[rows:, 0:steps] = (tail + dest.astype(jnp.float32)).astype(jnp.bfloat16)
    message_ref[rows:, steps:] = (tail + rank).astype(jnp.bfloat16)
    for copy in copies:
        copy.wait()


def part_kernel(n_panel, n_obs, cap, quads, which, last, *refs):
    buffers, pieces = dict(zip(which, refs)), refs[len(which) : len(which) + n_panel]
    rest, acc_ref = refs[len(which) + n_panel : -1], refs[-1]
    count = n_panel * n_obs
    me_p = lax.axis_index("panel")
    me_o = lax.axis_index("obs")
    rows = refs[0].shape[0] // (n_obs // 4) - EXTRA
    steps = refs[0].shape[1] // 2
    per = 16 // cap
    width = n_obs * cap
    depth = n_obs * width
    acc_ref[...] = jnp.zeros_like(acc_ref)
    if last:
        acc_ref[0:steps] = rest[0][...]
    slot_ids = lax.broadcasted_iota(jnp.int32, (count * 16, per * rows), 0)
    groups, starts = [], []
    for quad in quads:
        values, places = [], []
        for i in range(per):
            j = quad * per + i
            ref, base = buffers[j % 4], (j // 4) * (rows + EXTRA)
            tail = ref[base + rows : base + rows + EXTRA, :].astype(jnp.float32)[0:1].astype(jnp.int32)
            dest, rank = tail[:, 0:rows], tail[:, steps : steps + rows]
            within = ((me_o % per) ^ i) * cap + rank
            places.append((dest ^ (me_p * n_obs)) * 16 + within)
            values.append(ref[base : base + rows, :])
        pick = (slot_ids == jnp.concatenate(places, axis=1)).astype(jnp.bfloat16)
        groups.append(dot(pick, jnp.concatenate(values, axis=0)).astype(jnp.bfloat16))
        starts.append(((me_o // per) ^ quad) * 16)
    for k in range(n_panel):
        delays = pieces[k][2 * depth : 2 * depth + EXTRA, :].astype(jnp.float32)[0:1].astype(jnp.int32)
        for b in range(n_obs // 2):
            row = 32 * (k * (n_obs // 2) + b)
            source = jnp.concatenate(
                [g[row : row + 32, c * steps : (c + 1) * steps] for c in range(2) for g in groups], axis=0
            )
            weights = jnp.concatenate(
                [
                    pieces[k][pl.ds(pl.multiple_of(c * depth + (2 * b + h) * width + start, 16), 16), :]
                    for c in range(2)
                    for start in starts
                    for h in range(2)
                ],
                axis=0,
            )
            acc_ref[pl.ds(delays[0, b], steps), :] += dot(source.T, weights)
    if not last:
        rest[0][...] = acc_ref[0:steps]
        return
    share = steps // n_panel
    for k in range(n_panel):
        start = pl.multiple_of((me_p ^ k) * share, share)
        rest[1 + k][...] = acc_ref[pl.ds(start, share), :]


def per_device(les_rows, les_dest, loading_weight, thickness_weight, delays):
    n_panel = lax.axis_size("panel")
    n_obs = lax.axis_size("obs")
    count = n_panel * n_obs
    rows, _, steps = les_rows.shape
    cap = 2 * rows // count
    observers = loading_weight.shape[1]
    width = n_obs * cap
    nblocks = n_obs // 2
    params = pltpu.CompilerParams(vmem_limit_bytes=VMEM_LIMIT)
    vmem = pl.BlockSpec(memory_space=pltpu.VMEM)
    hbm = pl.BlockSpec(memory_space=pltpu.HBM)

    def along_panel(value, k):
        return lax.ppermute(value, "panel", [(i, i ^ k) for i in range(n_panel)])

    def along_obs(value, k):
        return lax.ppermute(value, "obs", [(i, i ^ k) for i in range(n_obs)])

    load = loading_weight.reshape(n_obs, n_panel, width, observers)
    thick = thickness_weight.reshape(n_obs, n_panel, width, observers)
    piece = jax.ShapeDtypeStruct((2 * n_obs * width + EXTRA, observers), jnp.bfloat16)
    message, own, to_c, to_x, to_xc = pl.pallas_call(
        functools.partial(pack_kernel, n_panel, n_obs, cap),
        out_shape=[jax.ShapeDtypeStruct((rows + EXTRA, 2 * steps), jnp.bfloat16)] + [piece] * n_panel,
        in_specs=[hbm] * 5,
        out_specs=[vmem] * (1 + n_panel),
        scratch_shapes=[
            pltpu.VMEM((2 * rows, steps), jnp.bfloat16),
            pltpu.VMEM((1, rows), jnp.int32),
            pltpu.SMEM((1, nblocks), jnp.int32),
            pltpu.SemaphoreType.DMA((n_panel, 2)),
            pltpu.SemaphoreType.DMA((3,)),
        ],
        compiler_params=params,
    )(
        *(
            pltpu.with_memory_space_constraint(value, pltpu.HBM)
            for value in (
                les_rows.reshape(2 * rows, steps),
                les_dest.reshape(1, rows),
                delays.reshape(1, nblocks),
                load,
                thick,
            )
        )
    )
    from_x, from_xc, from_c = along_panel(to_x, 2), along_panel(to_xc, 3), along_panel(to_c, 1)
    a = jnp.concatenate([message] + [along_obs(message, k) for k in range(4, n_obs, 4)], axis=0)
    a, from_c = lax.optimization_barrier((a, from_c))
    b, ya, yb = along_obs(a, 2), along_obs(a, 1), along_obs(a, 3)

    buffers, pieces = (a, ya, b, yb), (own, from_c, from_x, from_xc)
    per = 16 // cap
    share = jax.ShapeDtypeStruct((steps // n_panel, observers), jnp.float32)
    shares = []
    for last in (False, True):
        quads = [q for q in range(n_obs // per) if q % 2 == last]
        which = sorted({j % 4 for q in quads for j in range(q * per, (q + 1) * per)})
        shares = pl.pallas_call(
            functools.partial(part_kernel, n_panel, n_obs, cap, quads, which, last),
            out_shape=[share] * n_panel if last else [jax.ShapeDtypeStruct((steps, observers), jnp.float32)],
            in_specs=[vmem] * (len(which) + n_panel + last),
            out_specs=[vmem] * (n_panel if last else 1),
            scratch_shapes=[pltpu.VMEM((2 * steps, observers), jnp.float32)],
            compiler_params=params,
        )(*(buffers[w] for w in which), *pieces, *shares)
    total = shares[0]
    for k in (2, 3, 1):
        total = total + along_panel(shares[k], k)
    return total


def solution(mesh):
    placed = (
        P(("panel", "obs"), None, None),
        P(("panel", "obs"), None),
        P("panel", "obs"),
        P("panel", "obs"),
        P("panel", "obs"),
    )
    return jax.shard_map(
        per_device, mesh=mesh, in_specs=placed, out_specs=P("panel", "obs"), check_vma=False
    )
```

```python
import functools

import jax
import jax.numpy as jnp
from jax import lax
from jax.experimental import pallas as pl
from jax.experimental.pallas import tpu as pltpu
from jax.sharding import PartitionSpec as P

PBLK = 512
PACK_ORDER = (2, 3, 1, 0)
F_JOIN, F_LATE, F_NEAR = 4000000000, 10000000000, 2000000000
EXTRA = 16
VMEM_LIMIT = 48 * 1024 * 1024


def dot(a, b):
    return lax.dot_general(a, b, (((1,), (0,)), ((), ())), preferred_element_type=jnp.float32)


def pack_kernel(n_panel, n_obs, cap, rows_ref, dest_ref, delay_ref, load_ref, thick_ref, *refs):
    message_ref, pieces = refs[0], refs[1 : 1 + n_panel]
    rows_in, dest_in, delay_in, sems, few = refs[1 + n_panel :]
    count = n_panel * n_obs
    me_p = lax.axis_index("panel")
    width = n_obs * cap
    depth = n_obs * width
    small = [
        pltpu.make_async_copy(src, dst, few.at[i])
        for i, (src, dst) in enumerate(((rows_ref, rows_in), (dest_ref, dest_in), (delay_ref, delay_in)))
    ]
    for copy in small:
        copy.start()
    copies = []
    for k in PACK_ORDER:
        for i, ref in enumerate((load_ref, thick_ref)):
            there = pieces[k].at[pl.ds(i * depth, depth)].reshape(n_obs, width, ref.shape[3])
            copies.append(pltpu.make_async_copy(ref.at[:, me_p ^ k], there, sems.at[k, i]))
            copies[-1].start()
    rows, steps = rows_ref.shape[0] // 2, rows_ref.shape[1]
    nblocks = delay_ref.shape[1]
    for copy in small:
        copy.wait()
    lane = lax.broadcasted_iota(jnp.int32, (EXTRA, load_ref.shape[3]), 1)
    late = jnp.zeros(lane.shape, jnp.int32)
    for b in range(nblocks):
        late = jnp.where(lane == b, delay_in[0, b], late)
    for k in range(n_panel):
        pieces[k][2 * depth : 2 * depth + EXTRA, :] = late.astype(jnp.float32).astype(jnp.bfloat16)
    r0 = lax.broadcasted_iota(jnp.int32, (rows, 2 * rows), 0)
    r1 = lax.broadcasted_iota(jnp.int32, (rows, 2 * rows), 1)
    value = rows_in[...]
    pressure = dot((r1 == 2 * r0).astype(jnp.bfloat16), value).astype(jnp.bfloat16)
    velocity = dot((r1 == 2 * r0 + 1).astype(jnp.bfloat16), value).astype(jnp.bfloat16)
    t0 = lax.broadcasted_iota(jnp.int32, (steps, steps), 0)
    t1 = lax.broadcasted_iota(jnp.int32, (steps, steps), 1)
    slope = jnp.where(t0 == t1 + 1, 0.5, jnp.where(t0 == t1 - 1, -0.5, 0.0)).astype(jnp.bfloat16)
    message_ref[0:rows, 0:steps] = pressure
    message_ref[0:rows, steps:] = dot(velocity, slope).astype(jnp.bfloat16)
    dest = dest_in[...]
    onehot = lax.broadcasted_iota(jnp.int32, (count, rows), 0) == dest
    q0 = lax.broadcasted_iota(jnp.int32, (rows, rows), 0)
    q1 = lax.broadcasted_iota(jnp.int32, (rows, rows), 1)
    before = dot(onehot.astype(jnp.bfloat16), (q0 < q1).astype(jnp.bfloat16))
    rank = jnp.sum(jnp.where(onehot, before, 0.0), axis=0, keepdims=True)
    tail = jnp.zeros((EXTRA, steps), jnp.float32)
    message_ref[rows:, 0:steps] = (tail + dest.astype(jnp.float32)).astype(jnp.bfloat16)
    message_ref[rows:, steps:] = (tail + rank).astype(jnp.bfloat16)
    for copy in copies:
        copy.wait()


def late_kernel(*refs):
    for i, ref in enumerate(refs[:-1]):
        tail = ref[ref.shape[0] - EXTRA :, :].astype(jnp.float32)[0:8]
        refs[-1][8 * i : 8 * i + 8] = tail.astype(jnp.int32)


def join_kernel(*refs):
    at = 0
    for ref in refs[:-1]:
        refs[-1][at : at + ref.shape[0]] = ref[...]
        at += ref.shape[0]


def add_terms(n_obs, width, sources, pieces, delays, acc_ref):
    steps = sources[0].shape[1]
    depth = n_obs * width
    for source, piece, late in zip(sources, pieces, delays):
        for b in range(n_obs // 2):
            lo, hi = 2 * width * b, 2 * width * (b + 1)
            weights = jnp.concatenate([piece[lo:hi], piece[depth + lo : depth + hi]], axis=0)
            acc_ref[pl.ds(late[0, b], steps), :] += dot(source[b], weights)


def late_row(piece):
    return piece[piece.shape[0] - EXTRA :, :].astype(jnp.float32)[0:1].astype(jnp.int32)


def near_kernel(n_panel, n_obs, cap, a_ref, ya_ref, b_ref, yb_ref, own_ref, c_ref, near_ref, *refs):
    outs, (slots_ref, mine_ref, acc_ref) = refs[: n_panel - 2], refs[n_panel - 2 :]
    count = n_panel * n_obs
    me_p = lax.axis_index("panel")
    me_o = lax.axis_index("obs")
    rows = a_ref.shape[0] // (n_obs // 4) - EXTRA
    steps = a_ref.shape[1] // 2
    per = 16 // cap
    width = n_obs * cap
    slot_ids = lax.broadcasted_iota(jnp.int32, (count * 16, per * rows), 0)
    for quad in range(n_obs // per):
        values, places = [], []
        for i in range(per):
            j = quad * per + i
            ref, base = (a_ref, ya_ref, b_ref, yb_ref)[j % 4], (j // 4) * (rows + EXTRA)
            tail = ref[base + rows : base + rows + EXTRA, :].astype(jnp.float32)[0:1].astype(jnp.int32)
            dest, rank = tail[:, 0:rows], tail[:, steps : steps + rows]
            within = ((me_o % per) ^ i) * cap + rank
            places.append((dest ^ (me_p * n_obs)) * 16 + within)
            values.append(ref[base : base + rows, :])
        pick = (slot_ids == jnp.concatenate(places, axis=1)).astype(jnp.bfloat16)
        got = dot(pick, jnp.concatenate(values, axis=0)).astype(jnp.bfloat16)
        start = pl.multiple_of(((me_o // per) ^ quad) * 16, 16)
        slots_ref[:, pl.ds(start, 16), :] = got.reshape(count, 16, 2 * steps)
    for k in range(n_panel):
        for b in range(n_obs // 2):
            at = k * n_obs + 2 * b
            block = slots_ref[at : at + 2].reshape(2 * width, 2 * steps)
            into = mine_ref.at[k * (n_obs // 2) + b] if k < 2 else outs[k - 2].at[b]
            into[:, 0 : 2 * width] = block[:, 0:steps].T
            into[:, 2 * width :] = block[:, steps:].T
    acc_ref[...] = jnp.zeros_like(acc_ref)
    mine = [mine_ref.at[k * (n_obs // 2) : (k + 1) * (n_obs // 2)] for k in range(2)]
    add_terms(n_obs, width, mine, (own_ref, c_ref), (late_row(own_ref), late_row(c_ref)), acc_ref)
    near_ref[...] = acc_ref[0:steps]


def far_kernel(n_panel, n_obs, width, near_ref, *refs):
    far = n_panel - 2
    sources, pieces, late_ref = refs[:far], refs[far : 2 * far], refs[2 * far]
    outs, acc_ref = refs[2 * far + 1 : -1], refs[-1]
    me_p = lax.axis_index("panel")
    steps = near_ref.shape[0]
    acc_ref[0:steps] = near_ref[...]
    acc_ref[steps:] = jnp.zeros_like(acc_ref[steps:])
    delays = [late_ref[8 * k : 8 * k + 8][0:1] for k in range(far)]
    add_terms(n_obs, width, sources, pieces, delays, acc_ref)
    share = steps // n_panel
    for k in range(n_panel):
        start = pl.multiple_of((me_p ^ k) * share, share)
        outs[k][...] = acc_ref[pl.ds(start, share), :]


def per_device(les_rows, les_dest, loading_weight, thickness_weight, delays):
    n_panel = lax.axis_size("panel")
    n_obs = lax.axis_size("obs")
    count = n_panel * n_obs
    rows, _, steps = les_rows.shape
    cap = 2 * rows // count
    observers = loading_weight.shape[1]
    width = n_obs * cap
    nblocks = n_obs // 2
    params = pltpu.CompilerParams(vmem_limit_bytes=VMEM_LIMIT)
    vmem = pl.BlockSpec(memory_space=pltpu.VMEM)
    hbm = pl.BlockSpec(memory_space=pltpu.HBM)

    def along_panel(value, k):
        return lax.ppermute(value, "panel", [(i, i ^ k) for i in range(n_panel)])

    def along_obs(value, k):
        return lax.ppermute(value, "obs", [(i, i ^ k) for i in range(n_obs)])

    load = loading_weight.reshape(n_obs, n_panel, width, observers)
    thick = thickness_weight.reshape(n_obs, n_panel, width, observers)
    piece = jax.ShapeDtypeStruct((2 * n_obs * width + EXTRA, observers), jnp.bfloat16)
    message, own, to_c, to_x, to_xc = pl.pallas_call(
        functools.partial(pack_kernel, n_panel, n_obs, cap),
        out_shape=[jax.ShapeDtypeStruct((rows + EXTRA, 2 * steps), jnp.bfloat16)] + [piece] * n_panel,
        in_specs=[hbm] * 5,
        out_specs=[vmem] * (1 + n_panel),
        scratch_shapes=[
            pltpu.VMEM((2 * rows, steps), jnp.bfloat16),
            pltpu.VMEM((1, rows), jnp.int32),
            pltpu.SMEM((1, nblocks), jnp.int32),
            pltpu.SemaphoreType.DMA((n_panel, 2)),
            pltpu.SemaphoreType.DMA((3,)),
        ],
        compiler_params=params,
    )(
        *(
            pltpu.with_memory_space_constraint(value, pltpu.HBM)
            for value in (
                les_rows.reshape(2 * rows, steps),
                les_dest.reshape(1, rows),
                delays.reshape(1, nblocks),
                load,
                thick,
            )
        )
    )
    from_x, from_xc, from_c = along_panel(to_x, 2), along_panel(to_xc, 3), along_panel(to_c, 1)
    ranges = range(4, n_obs, 4)
    far = [along_obs(message, k) for k in ranges]
    later, from_c = lax.optimization_barrier((message, from_c))
    near = along_obs(later, 3)
    a = pl.pallas_call(
        join_kernel,
        out_shape=jax.ShapeDtypeStruct((n_obs // 4 * (rows + EXTRA), 2 * steps), jnp.bfloat16),
        in_specs=[vmem] * (n_obs // 4),
        out_specs=vmem,
        compiler_params=params,
        cost_estimate=pl.CostEstimate(flops=F_JOIN, bytes_accessed=0, transcendentals=0),
    )(message, *far)
    ya, b = along_obs(a, 1), along_obs(a, 2)
    again, near = lax.optimization_barrier((jnp.concatenate(far, axis=0), near))
    yb = jnp.concatenate([near, along_obs(again, 3)], axis=0)

    acc = pltpu.VMEM((2 * steps, observers), jnp.float32)
    source = jax.ShapeDtypeStruct((nblocks, steps, 4 * width), jnp.bfloat16)
    near, *sources = pl.pallas_call(
        functools.partial(near_kernel, n_panel, n_obs, cap),
        out_shape=[jax.ShapeDtypeStruct((steps, observers), jnp.float32)] + [source] * (n_panel - 2),
        in_specs=[vmem] * 6,
        out_specs=[vmem] * (n_panel - 1),
        scratch_shapes=[
            pltpu.VMEM((count, width, 2 * steps), jnp.bfloat16),
            pltpu.VMEM((2 * nblocks, steps, 4 * width), jnp.bfloat16),
            acc,
        ],
        compiler_params=params,
        cost_estimate=pl.CostEstimate(flops=F_NEAR, bytes_accessed=0, transcendentals=0),
    )(a, ya, b, yb, own, from_c)
    pieces = (from_x, from_xc)
    late = pl.pallas_call(
        late_kernel,
        out_shape=jax.ShapeDtypeStruct((8 * len(pieces), observers), jnp.int32),
        in_specs=[vmem] * len(pieces),
        out_specs=vmem,
        compiler_params=params,
        cost_estimate=pl.CostEstimate(flops=F_LATE, bytes_accessed=0, transcendentals=0),
    )(*pieces)
    shares = pl.pallas_call(
        functools.partial(far_kernel, n_panel, n_obs, width),
        out_shape=[jax.ShapeDtypeStruct((steps // n_panel, observers), jnp.float32)] * n_panel,
        in_specs=[vmem] * (2 + 2 * len(pieces)),
        out_specs=[vmem] * n_panel,
        scratch_shapes=[acc],
        compiler_params=params,
    )(near, *sources, *pieces, late)
    total = shares[0]
    for k in (2, 3, 1):
        total = total + along_panel(shares[k], k)
    return total


def solution(mesh):
    placed = (
        P(("panel", "obs"), None, None),
        P(("panel", "obs"), None),
        P("panel", "obs"),
        P("panel", "obs"),
        P("panel", "obs"),
    )
    return jax.shard_map(
        per_device, mesh=mesh, in_specs=placed, out_specs=P("panel", "obs"), check_vma=False
    )
```

```python
import functools

import jax
import jax.numpy as jnp
from jax import lax
from jax.experimental import pallas as pl
from jax.experimental.pallas import tpu as pltpu
from jax.sharding import PartitionSpec as P

PBLK = 512
PACK_ORDER = (2, 3, 1, 0)
EXTRA = 16
VMEM_LIMIT = 48 * 1024 * 1024


def dot(a, b):
    return lax.dot_general(a, b, (((1,), (0,)), ((), ())), preferred_element_type=jnp.float32)


def pack_kernel(n_panel, n_obs, cap, rows_ref, dest_ref, delay_ref, load_ref, thick_ref, *refs):
    message_ref, pieces = refs[0], refs[1 : 1 + n_panel]
    rows_in, dest_in, delay_in, sems, few = refs[1 + n_panel :]
    count = n_panel * n_obs
    me_p = lax.axis_index("panel")
    width = n_obs * cap
    depth = n_obs * width
    small = [
        pltpu.make_async_copy(src, dst, few.at[i])
        for i, (src, dst) in enumerate(((rows_ref, rows_in), (dest_ref, dest_in), (delay_ref, delay_in)))
    ]
    for copy in small:
        copy.start()
    copies = []
    for k in PACK_ORDER:
        for i, ref in enumerate((load_ref, thick_ref)):
            there = pieces[k].at[pl.ds(i * depth, depth)].reshape(n_obs, width, ref.shape[3])
            copies.append(pltpu.make_async_copy(ref.at[:, me_p ^ k], there, sems.at[k, i]))
            copies[-1].start()
    rows, steps = rows_ref.shape[0] // 2, rows_ref.shape[1]
    nblocks = delay_ref.shape[1]
    for copy in small:
        copy.wait()
    lane = lax.broadcasted_iota(jnp.int32, (EXTRA, load_ref.shape[3]), 1)
    late = jnp.zeros(lane.shape, jnp.int32)
    for b in range(nblocks):
        late = jnp.where(lane == b, delay_in[0, b], late)
    for k in range(n_panel):
        pieces[k][2 * depth : 2 * depth + EXTRA, :] = late.astype(jnp.float32).astype(jnp.bfloat16)
    r0 = lax.broadcasted_iota(jnp.int32, (rows, 2 * rows), 0)
    r1 = lax.broadcasted_iota(jnp.int32, (rows, 2 * rows), 1)
    value = rows_in[...]
    pressure = dot((r1 == 2 * r0).astype(jnp.bfloat16), value).astype(jnp.bfloat16)
    velocity = dot((r1 == 2 * r0 + 1).astype(jnp.bfloat16), value).astype(jnp.bfloat16)
    t0 = lax.broadcasted_iota(jnp.int32, (steps, steps), 0)
    t1 = lax.broadcasted_iota(jnp.int32, (steps, steps), 1)
    slope = jnp.where(t0 == t1 + 1, 0.5, jnp.where(t0 == t1 - 1, -0.5, 0.0)).astype(jnp.bfloat16)
    message_ref[0:rows, 0:steps] = pressure
    message_ref[0:rows, steps:] = dot(velocity, slope).astype(jnp.bfloat16)
    dest = dest_in[...]
    onehot = lax.broadcasted_iota(jnp.int32, (count, rows), 0) == dest
    q0 = lax.broadcasted_iota(jnp.int32, (rows, rows), 0)
    q1 = lax.broadcasted_iota(jnp.int32, (rows, rows), 1)
    before = dot(onehot.astype(jnp.bfloat16), (q0 < q1).astype(jnp.bfloat16))
    rank = jnp.sum(jnp.where(onehot, before, 0.0), axis=0, keepdims=True)
    tail = jnp.zeros((EXTRA, steps), jnp.float32)
    message_ref[rows:, 0:steps] = (tail + dest.astype(jnp.float32)).astype(jnp.bfloat16)
    message_ref[rows:, steps:] = (tail + rank).astype(jnp.bfloat16)
    for copy in copies:
        copy.wait()


def late_kernel(*refs):
    for i, ref in enumerate(refs[:-1]):
        tail = ref[ref.shape[0] - EXTRA :, :].astype(jnp.float32)[0:8]
        refs[-1][8 * i : 8 * i + 8] = tail.astype(jnp.int32)


def join_kernel(*refs):
    at = 0
    for ref in refs[:-1]:
        refs[-1][at : at + ref.shape[0]] = ref[...]
        at += ref.shape[0]


def part_kernel(n_panel, n_obs, cap, quads, which, last, *refs):
    buffers, pieces = dict(zip(which, refs)), refs[len(which) : len(which) + n_panel]
    late_ref, rest, acc_ref = refs[len(which) + n_panel], refs[len(which) + n_panel + 1 : -1], refs[-1]
    count = n_panel * n_obs
    me_p = lax.axis_index("panel")
    me_o = lax.axis_index("obs")
    rows = refs[0].shape[0] // (n_obs // 4) - EXTRA
    steps = refs[0].shape[1] // 2
    per = 16 // cap
    width = n_obs * cap
    depth = n_obs * width
    acc_ref[...] = jnp.zeros_like(acc_ref)
    if last:
        acc_ref[0:steps] = rest[0][...]
    slot_ids = lax.broadcasted_iota(jnp.int32, (count * 16, per * rows), 0)
    groups, starts = [], []
    for quad in quads:
        values, places = [], []
        for i in range(per):
            j = quad * per + i
            ref, base = buffers[j % 4], (j // 4) * (rows + EXTRA)
            tail = ref[base + rows : base + rows + EXTRA, :].astype(jnp.float32)[0:1].astype(jnp.int32)
            dest, rank = tail[:, 0:rows], tail[:, steps : steps + rows]
            within = ((me_o % per) ^ i) * cap + rank
            places.append((dest ^ (me_p * n_obs)) * 16 + within)
            values.append(ref[base : base + rows, :])
        pick = (slot_ids == jnp.concatenate(places, axis=1)).astype(jnp.bfloat16)
        groups.append(dot(pick, jnp.concatenate(values, axis=0)).astype(jnp.bfloat16))
        starts.append(((me_o // per) ^ quad) * 16)
    for k in range(n_panel):
        delays = late_ref[8 * k : 8 * k + 8][0:1]
        for b in range(n_obs // 2):
            row = 32 * (k * (n_obs // 2) + b)
            source = jnp.concatenate(
                [g[row : row + 32, c * steps : (c + 1) * steps] for c in range(2) for g in groups], axis=0
            )
            weights = jnp.concatenate(
                [
                    pieces[k][pl.ds(pl.multiple_of(c * depth + (2 * b + h) * width + start, 16), 16), :]
                    for c in range(2)
                    for start in starts
                    for h in range(2)
                ],
                axis=0,
            )
            acc_ref[pl.ds(delays[0, b], steps), :] += dot(source.T, weights)
    if not last:
        rest[0][...] = acc_ref[0:steps]
        return
    share = steps // n_panel
    for k in range(n_panel):
        start = pl.multiple_of((me_p ^ k) * share, share)
        rest[1 + k][...] = acc_ref[pl.ds(start, share), :]


def per_device(les_rows, les_dest, loading_weight, thickness_weight, delays):
    n_panel = lax.axis_size("panel")
    n_obs = lax.axis_size("obs")
    count = n_panel * n_obs
    rows, _, steps = les_rows.shape
    cap = 2 * rows // count
    observers = loading_weight.shape[1]
    width = n_obs * cap
    nblocks = n_obs // 2
    params = pltpu.CompilerParams(vmem_limit_bytes=VMEM_LIMIT)
    vmem = pl.BlockSpec(memory_space=pltpu.VMEM)
    hbm = pl.BlockSpec(memory_space=pltpu.HBM)

    def along_panel(value, k):
        return lax.ppermute(value, "panel", [(i, i ^ k) for i in range(n_panel)])

    def along_obs(value, k):
        return lax.ppermute(value, "obs", [(i, i ^ k) for i in range(n_obs)])

    load = loading_weight.reshape(n_obs, n_panel, width, observers)
    thick = thickness_weight.reshape(n_obs, n_panel, width, observers)
    piece = jax.ShapeDtypeStruct((2 * n_obs * width + EXTRA, observers), jnp.bfloat16)
    message, own, to_c, to_x, to_xc = pl.pallas_call(
        functools.partial(pack_kernel, n_panel, n_obs, cap),
        out_shape=[jax.ShapeDtypeStruct((rows + EXTRA, 2 * steps), jnp.bfloat16)] + [piece] * n_panel,
        in_specs=[hbm] * 5,
        out_specs=[vmem] * (1 + n_panel),
        scratch_shapes=[
            pltpu.VMEM((2 * rows, steps), jnp.bfloat16),
            pltpu.VMEM((1, rows), jnp.int32),
            pltpu.SMEM((1, nblocks), jnp.int32),
            pltpu.SemaphoreType.DMA((n_panel, 2)),
            pltpu.SemaphoreType.DMA((3,)),
        ],
        compiler_params=params,
    )(
        *(
            pltpu.with_memory_space_constraint(value, pltpu.HBM)
            for value in (
                les_rows.reshape(2 * rows, steps),
                les_dest.reshape(1, rows),
                delays.reshape(1, nblocks),
                load,
                thick,
            )
        )
    )
    from_x, from_xc, from_c = along_panel(to_x, 2), along_panel(to_xc, 3), along_panel(to_c, 1)
    ranges = range(4, n_obs, 4)
    far = [along_obs(message, k) for k in ranges]
    later, from_c = lax.optimization_barrier((message, from_c))
    near = along_obs(later, 3)
    a = pl.pallas_call(
        join_kernel,
        out_shape=jax.ShapeDtypeStruct((n_obs // 4 * (rows + EXTRA), 2 * steps), jnp.bfloat16),
        in_specs=[vmem] * (n_obs // 4),
        out_specs=vmem,
        compiler_params=params,
        cost_estimate=pl.CostEstimate(flops=4*10**9, bytes_accessed=0, transcendentals=0),
    )(message, *far)
    ya, b = along_obs(a, 1), along_obs(a, 2)
    again, near = lax.optimization_barrier((jnp.concatenate(far, axis=0), near))
    yb = jnp.concatenate([near, along_obs(again, 3)], axis=0)

    buffers, pieces = (a, ya, b, yb), (own, from_c, from_x, from_xc)
    per = 16 // cap
    late = pl.pallas_call(
        late_kernel,
        out_shape=jax.ShapeDtypeStruct((8 * n_panel, observers), jnp.int32),
        in_specs=[vmem] * n_panel,
        out_specs=vmem,
        compiler_params=params,
        cost_estimate=pl.CostEstimate(flops=2*10**9, bytes_accessed=0, transcendentals=0),
    )(*pieces)
    share = jax.ShapeDtypeStruct((steps // n_panel, observers), jnp.float32)
    shares = []
    for last in (False, True):
        quads = [q for q in range(n_obs // per) if q % 2 == last]
        which = sorted({j % 4 for q in quads for j in range(q * per, (q + 1) * per)})
        shares = pl.pallas_call(
            functools.partial(part_kernel, n_panel, n_obs, cap, quads, which, last),
            out_shape=[share] * n_panel if last else [jax.ShapeDtypeStruct((steps, observers), jnp.float32)],
            in_specs=[vmem] * (len(which) + n_panel + 1 + last),
            out_specs=[vmem] * (n_panel if last else 1),
            scratch_shapes=[pltpu.VMEM((2 * steps, observers), jnp.float32)],
            compiler_params=params,
        )(*(buffers[w] for w in which), *pieces, late, *shares)
    total = shares[0]
    for k in (3, 1, 2):
        total = total + along_panel(shares[k], k)
    return total


def solution(mesh):
    placed = (
        P(("panel", "obs"), None, None),
        P(("panel", "obs"), None),
        P("panel", "obs"),
        P("panel", "obs"),
        P("panel", "obs"),
    )
    return jax.shard_map(
        per_device, mesh=mesh, in_specs=placed, out_specs=P("panel", "obs"), check_vma=False
    )
```

```python
import functools

import jax
import jax.numpy as jnp
from jax import lax
from jax.experimental import pallas as pl
from jax.experimental.pallas import tpu as pltpu
from jax.sharding import PartitionSpec as P

PBLK = 512
PACK_ORDER = (2, 3, 1, 0)
EXTRA = 16
VMEM_LIMIT = 48 * 1024 * 1024


def dot(a, b):
    return lax.dot_general(a, b, (((1,), (0,)), ((), ())), preferred_element_type=jnp.float32)


def pack_kernel(n_panel, n_obs, cap, rows_ref, dest_ref, delay_ref, load_ref, thick_ref, *refs):
    message_ref, pieces = refs[0], refs[1 : 1 + n_panel]
    rows_in, dest_in, delay_in, sems, few = refs[1 + n_panel :]
    count = n_panel * n_obs
    me_p = lax.axis_index("panel")
    width = n_obs * cap
    depth = n_obs * width
    small = [
        pltpu.make_async_copy(src, dst, few.at[i])
        for i, (src, dst) in enumerate(((rows_ref, rows_in), (dest_ref, dest_in), (delay_ref, delay_in)))
    ]
    for copy in small:
        copy.start()
    copies = []
    for k in PACK_ORDER:
        for i, ref in enumerate((load_ref, thick_ref)):
            there = pieces[k].at[pl.ds(i * depth, depth)].reshape(n_obs, width, ref.shape[3])
            copies.append(pltpu.make_async_copy(ref.at[:, me_p ^ k], there, sems.at[k, i]))
            copies[-1].start()
    rows, steps = rows_ref.shape[0] // 2, rows_ref.shape[1]
    nblocks = delay_ref.shape[1]
    for copy in small:
        copy.wait()
    lane = lax.broadcasted_iota(jnp.int32, (EXTRA, load_ref.shape[3]), 1)
    late = jnp.zeros(lane.shape, jnp.int32)
    for b in range(nblocks):
        late = jnp.where(lane == b, delay_in[0, b], late)
    for k in range(n_panel):
        pieces[k][2 * depth : 2 * depth + EXTRA, :] = late.astype(jnp.float32).astype(jnp.bfloat16)
    r0 = lax.broadcasted_iota(jnp.int32, (rows, 2 * rows), 0)
    r1 = lax.broadcasted_iota(jnp.int32, (rows, 2 * rows), 1)
    value = rows_in[...]
    pressure = dot((r1 == 2 * r0).astype(jnp.bfloat16), value).astype(jnp.bfloat16)
    velocity = dot((r1 == 2 * r0 + 1).astype(jnp.bfloat16), value).astype(jnp.bfloat16)
    t0 = lax.broadcasted_iota(jnp.int32, (steps, steps), 0)
    t1 = lax.broadcasted_iota(jnp.int32, (steps, steps), 1)
    slope = jnp.where(t0 == t1 + 1, 0.5, jnp.where(t0 == t1 - 1, -0.5, 0.0)).astype(jnp.bfloat16)
    message_ref[0:rows, 0:steps] = pressure
    message_ref[0:rows, steps:] = dot(velocity, slope).astype(jnp.bfloat16)
    dest = dest_in[...]
    onehot = lax.broadcasted_iota(jnp.int32, (count, rows), 0) == dest
    q0 = lax.broadcasted_iota(jnp.int32, (rows, rows), 0)
    q1 = lax.broadcasted_iota(jnp.int32, (rows, rows), 1)
    before = dot(onehot.astype(jnp.bfloat16), (q0 < q1).astype(jnp.bfloat16))
    rank = jnp.sum(jnp.where(onehot, before, 0.0), axis=0, keepdims=True)
    tail = jnp.zeros((EXTRA, steps), jnp.float32)
    message_ref[rows:, 0:steps] = (tail + dest.astype(jnp.float32)).astype(jnp.bfloat16)
    message_ref[rows:, steps:] = (tail + rank).astype(jnp.bfloat16)
    for copy in copies:
        copy.wait()


def late_kernel(*refs):
    for i, ref in enumerate(refs[:-1]):
        tail = ref[ref.shape[0] - EXTRA :, :].astype(jnp.float32)[0:8]
        refs[-1][8 * i : 8 * i + 8] = tail.astype(jnp.int32)


def join_kernel(*refs):
    at = 0
    for ref in refs[:-1]:
        refs[-1][at : at + ref.shape[0]] = ref[...]
        at += ref.shape[0]


def part_kernel(n_panel, n_obs, cap, *refs):
    buffers, pieces, late_ref = refs[:4], refs[4 : 4 + n_panel], refs[4 + n_panel]
    outs, acc_ref = refs[5 + n_panel : -1], refs[-1]
    count = n_panel * n_obs
    me_p = lax.axis_index("panel")
    me_o = lax.axis_index("obs")
    rows = refs[0].shape[0] // (n_obs // 4) - EXTRA
    steps = refs[0].shape[1] // 2
    per = 16 // cap
    width = n_obs * cap
    depth = n_obs * width
    acc_ref[...] = jnp.zeros_like(acc_ref)
    slot_ids = lax.broadcasted_iota(jnp.int32, (count * 16, per * rows), 0)
    groups, starts = [], []
    for quad in range(n_obs // per):
        values, places = [], []
        for i in range(per):
            j = quad * per + i
            ref, base = buffers[j % 4], (j // 4) * (rows + EXTRA)
            tail = ref[base + rows : base + rows + EXTRA, :].astype(jnp.float32)[0:1].astype(jnp.int32)
            dest, rank = tail[:, 0:rows], tail[:, steps : steps + rows]
            within = ((me_o % per) ^ i) * cap + rank
            places.append((dest ^ (me_p * n_obs)) * 16 + within)
            values.append(ref[base : base + rows, :])
        pick = (slot_ids == jnp.concatenate(places, axis=1)).astype(jnp.bfloat16)
        groups.append(dot(pick, jnp.concatenate(values, axis=0)).astype(jnp.bfloat16))
        starts.append(((me_o // per) ^ quad) * 16)
    for k in range(n_panel):
        delays = late_ref[8 * k : 8 * k + 8][0:1]
        for b in range(n_obs // 2):
            row = 32 * (k * (n_obs // 2) + b)
            source = jnp.concatenate(
                [g[row : row + 32, c * steps : (c + 1) * steps] for c in range(2) for g in groups], axis=0
            )
            weights = jnp.concatenate(
                [
                    pieces[k][pl.ds(pl.multiple_of(c * depth + (2 * b + h) * width + start, 16), 16), :]
                    for c in range(2)
                    for start in starts
                    for h in range(2)
                ],
                axis=0,
            )
            acc_ref[pl.ds(delays[0, b], steps), :] += dot(source.T, weights)
    share = steps // n_panel
    for k in range(n_panel):
        start = pl.multiple_of((me_p ^ k) * share, share)
        outs[k][...] = acc_ref[pl.ds(start, share), :]


def per_device(les_rows, les_dest, loading_weight, thickness_weight, delays):
    n_panel = lax.axis_size("panel")
    n_obs = lax.axis_size("obs")
    count = n_panel * n_obs
    rows, _, steps = les_rows.shape
    cap = 2 * rows // count
    observers = loading_weight.shape[1]
    width = n_obs * cap
    nblocks = n_obs // 2
    params = pltpu.CompilerParams(vmem_limit_bytes=VMEM_LIMIT)
    vmem = pl.BlockSpec(memory_space=pltpu.VMEM)
    hbm = pl.BlockSpec(memory_space=pltpu.HBM)

    def along_panel(value, k):
        return lax.ppermute(value, "panel", [(i, i ^ k) for i in range(n_panel)])

    def along_obs(value, k):
        return lax.ppermute(value, "obs", [(i, i ^ k) for i in range(n_obs)])

    load = loading_weight.reshape(n_obs, n_panel, width, observers)
    thick = thickness_weight.reshape(n_obs, n_panel, width, observers)
    piece = jax.ShapeDtypeStruct((2 * n_obs * width + EXTRA, observers), jnp.bfloat16)
    message, own, to_c, to_x, to_xc = pl.pallas_call(
        functools.partial(pack_kernel, n_panel, n_obs, cap),
        out_shape=[jax.ShapeDtypeStruct((rows + EXTRA, 2 * steps), jnp.bfloat16)] + [piece] * n_panel,
        in_specs=[hbm] * 5,
        out_specs=[vmem] * (1 + n_panel),
        scratch_shapes=[
            pltpu.VMEM((2 * rows, steps), jnp.bfloat16),
            pltpu.VMEM((1, rows), jnp.int32),
            pltpu.SMEM((1, nblocks), jnp.int32),
            pltpu.SemaphoreType.DMA((n_panel, 2)),
            pltpu.SemaphoreType.DMA((3,)),
        ],
        compiler_params=params,
    )(
        *(
            pltpu.with_memory_space_constraint(value, pltpu.HBM)
            for value in (
                les_rows.reshape(2 * rows, steps),
                les_dest.reshape(1, rows),
                delays.reshape(1, nblocks),
                load,
                thick,
            )
        )
    )
    from_x, from_xc, from_c = along_panel(to_x, 2), along_panel(to_xc, 3), along_panel(to_c, 1)
    ranges = range(4, n_obs, 4)
    far = [along_obs(message, k) for k in ranges]
    later, from_c = lax.optimization_barrier((message, from_c))
    near = along_obs(later, 3)
    a = pl.pallas_call(
        join_kernel,
        out_shape=jax.ShapeDtypeStruct((n_obs // 4 * (rows + EXTRA), 2 * steps), jnp.bfloat16),
        in_specs=[vmem] * (n_obs // 4),
        out_specs=vmem,
        compiler_params=params,
        cost_estimate=pl.CostEstimate(flops=4*10**9, bytes_accessed=0, transcendentals=0),
    )(message, *far)
    ya, b = along_obs(a, 1), along_obs(a, 2)
    again, near = lax.optimization_barrier((jnp.concatenate(far, axis=0), near))
    yb = jnp.concatenate([near, along_obs(again, 3)], axis=0)

    buffers, pieces = (a, ya, b, yb), (own, from_c, from_x, from_xc)
    late = pl.pallas_call(
        late_kernel,
        out_shape=jax.ShapeDtypeStruct((8 * n_panel, observers), jnp.int32),
        in_specs=[vmem] * n_panel,
        out_specs=vmem,
        compiler_params=params,
        cost_estimate=pl.CostEstimate(flops=2*10**9, bytes_accessed=0, transcendentals=0),
    )(*pieces)
    share = jax.ShapeDtypeStruct((steps // n_panel, observers), jnp.float32)
    shares = pl.pallas_call(
        functools.partial(part_kernel, n_panel, n_obs, cap),
        out_shape=[share] * n_panel,
        in_specs=[vmem] * (5 + n_panel),
        out_specs=[vmem] * n_panel,
        scratch_shapes=[pltpu.VMEM((2 * steps, observers), jnp.float32)],
        compiler_params=params,
        cost_estimate=pl.CostEstimate(flops=1, bytes_accessed=0, transcendentals=0),
    )(*buffers, *pieces, late)
    total = shares[0]
    for k in (3, 1, 2):
        total = total + along_panel(shares[k], k)
    return total


def solution(mesh):
    placed = (
        P(("panel", "obs"), None, None),
        P(("panel", "obs"), None),
        P("panel", "obs"),
        P("panel", "obs"),
        P("panel", "obs"),
    )
    return jax.shard_map(
        per_device, mesh=mesh, in_specs=placed, out_specs=P("panel", "obs"), check_vma=False
    )
```

```python
import functools

import jax
import jax.numpy as jnp
from jax import lax
from jax.experimental import pallas as pl
from jax.experimental.pallas import tpu as pltpu
from jax.sharding import PartitionSpec as P

PBLK = 512
PACK_ORDER = (2, 3, 1, 0)
EXTRA = 16
VMEM_LIMIT = 48 * 1024 * 1024


def dot(a, b):
    return lax.dot_general(a, b, (((1,), (0,)), ((), ())), preferred_element_type=jnp.float32)


def pack_kernel(n_panel, n_obs, cap, rows_ref, dest_ref, delay_ref, load_ref, thick_ref, *refs):
    message_ref, pieces = refs[0], refs[1 : 1 + n_panel]
    rows_in, dest_in, delay_in, sems, few = refs[1 + n_panel :]
    count = n_panel * n_obs
    me_p = lax.axis_index("panel")
    width = n_obs * cap
    depth = n_obs * width
    small = [
        pltpu.make_async_copy(src, dst, few.at[i])
        for i, (src, dst) in enumerate(((rows_ref, rows_in), (dest_ref, dest_in), (delay_ref, delay_in)))
    ]
    for copy in small:
        copy.start()
    copies = []
    for k in PACK_ORDER:
        for i, ref in enumerate((load_ref, thick_ref)):
            there = pieces[k].at[pl.ds(i * depth, depth)].reshape(n_obs, width, ref.shape[3])
            copies.append(pltpu.make_async_copy(ref.at[:, me_p ^ k], there, sems.at[k, i]))
            copies[-1].start()
    rows, steps = rows_ref.shape[0] // 2, rows_ref.shape[1]
    nblocks = delay_ref.shape[1]
    for copy in small:
        copy.wait()
    lane = lax.broadcasted_iota(jnp.int32, (EXTRA, load_ref.shape[3]), 1)
    late = jnp.zeros(lane.shape, jnp.int32)
    for b in range(nblocks):
        late = jnp.where(lane == b, delay_in[0, b], late)
    for k in range(n_panel):
        pieces[k][2 * depth : 2 * depth + EXTRA, :] = late.astype(jnp.float32).astype(jnp.bfloat16)
    r0 = lax.broadcasted_iota(jnp.int32, (rows, 2 * rows), 0)
    r1 = lax.broadcasted_iota(jnp.int32, (rows, 2 * rows), 1)
    value = rows_in[...]
    pressure = dot((r1 == 2 * r0).astype(jnp.bfloat16), value).astype(jnp.bfloat16)
    velocity = dot((r1 == 2 * r0 + 1).astype(jnp.bfloat16), value).astype(jnp.bfloat16)
    t0 = lax.broadcasted_iota(jnp.int32, (steps, steps), 0)
    t1 = lax.broadcasted_iota(jnp.int32, (steps, steps), 1)
    slope = jnp.where(t0 == t1 + 1, 0.5, jnp.where(t0 == t1 - 1, -0.5, 0.0)).astype(jnp.bfloat16)
    message_ref[0:rows, 0:steps] = pressure
    message_ref[0:rows, steps:] = dot(velocity, slope).astype(jnp.bfloat16)
    dest = dest_in[...]
    onehot = lax.broadcasted_iota(jnp.int32, (count, rows), 0) == dest
    q0 = lax.broadcasted_iota(jnp.int32, (rows, rows), 0)
    q1 = lax.broadcasted_iota(jnp.int32, (rows, rows), 1)
    before = dot(onehot.astype(jnp.bfloat16), (q0 < q1).astype(jnp.bfloat16))
    rank = jnp.sum(jnp.where(onehot, before, 0.0), axis=0, keepdims=True)
    tail = jnp.zeros((EXTRA, steps), jnp.float32)
    message_ref[rows:, 0:steps] = (tail + dest.astype(jnp.float32)).astype(jnp.bfloat16)
    message_ref[rows:, steps:] = (tail + rank).astype(jnp.bfloat16)
    for copy in copies:
        copy.wait()


def late_kernel(*refs):
    for i, ref in enumerate(refs[:-1]):
        tail = ref[ref.shape[0] - EXTRA :, :].astype(jnp.float32)[0:8]
        refs[-1][8 * i : 8 * i + 8] = tail.astype(jnp.int32)


def join_kernel(*refs):
    at = 0
    for ref in refs[:-1]:
        refs[-1][at : at + ref.shape[0]] = ref[...]
        at += ref.shape[0]


def part_kernel(n_panel, n_obs, cap, *refs):
    buffers, pieces, late_ref = refs[:4], refs[4 : 4 + n_panel], refs[4 + n_panel]
    outs, acc_ref = refs[5 + n_panel : -1], refs[-1]
    count = n_panel * n_obs
    me_p = lax.axis_index("panel")
    me_o = lax.axis_index("obs")
    rows = refs[0].shape[0] // (n_obs // 4) - EXTRA
    steps = refs[0].shape[1] // 2
    per = 16 // cap
    width = n_obs * cap
    depth = n_obs * width
    acc_ref[...] = jnp.zeros_like(acc_ref)
    slot_ids = lax.broadcasted_iota(jnp.int32, (count * 16, per * rows), 0)
    groups, starts = [], []
    for quad in range(n_obs // per):
        values, places = [], []
        for i in range(per):
            j = quad * per + i
            ref, base = buffers[j % 4], (j // 4) * (rows + EXTRA)
            tail = ref[base + rows : base + rows + EXTRA, :].astype(jnp.float32)[0:1].astype(jnp.int32)
            dest, rank = tail[:, 0:rows], tail[:, steps : steps + rows]
            within = ((me_o % per) ^ i) * cap + rank
            places.append((dest ^ (me_p * n_obs)) * 16 + within)
            values.append(ref[base : base + rows, :])
        pick = (slot_ids == jnp.concatenate(places, axis=1)).astype(jnp.bfloat16)
        groups.append(dot(pick, jnp.concatenate(values, axis=0)).astype(jnp.bfloat16))
        starts.append(((me_o // per) ^ quad) * 16)
    for k in range(n_panel):
        if k < 2:
            delays = pieces[k][2 * depth : 2 * depth + EXTRA, :].astype(jnp.float32)[0:1].astype(jnp.int32)
        else:
            delays = late_ref[8 * (k - 2) : 8 * (k - 1)][0:1]
        for b in range(n_obs // 2):
            row = 32 * (k * (n_obs // 2) + b)
            source = jnp.concatenate(
                [g[row : row + 32, c * steps : (c + 1) * steps] for c in range(2) for g in groups], axis=0
            )
            weights = jnp.concatenate(
                [
                    pieces[k][pl.ds(pl.multiple_of(c * depth + (2 * b + h) * width + start, 16), 16), :]
                    for c in range(2)
                    for start in starts
                    for h in range(2)
                ],
                axis=0,
            )
            acc_ref[pl.ds(delays[0, b], steps), :] += dot(source.T, weights)
    share = steps // n_panel
    for k in range(n_panel):
        start = pl.multiple_of((me_p ^ k) * share, share)
        outs[k][...] = acc_ref[pl.ds(start, share), :]


def per_device(les_rows, les_dest, loading_weight, thickness_weight, delays):
    n_panel = lax.axis_size("panel")
    n_obs = lax.axis_size("obs")
    count = n_panel * n_obs
    rows, _, steps = les_rows.shape
    cap = 2 * rows // count
    observers = loading_weight.shape[1]
    width = n_obs * cap
    nblocks = n_obs // 2
    params = pltpu.CompilerParams(vmem_limit_bytes=VMEM_LIMIT)
    vmem = pl.BlockSpec(memory_space=pltpu.VMEM)
    hbm = pl.BlockSpec(memory_space=pltpu.HBM)

    def along_panel(value, k):
        return lax.ppermute(value, "panel", [(i, i ^ k) for i in range(n_panel)])

    def along_obs(value, k):
        return lax.ppermute(value, "obs", [(i, i ^ k) for i in range(n_obs)])

    load = loading_weight.reshape(n_obs, n_panel, width, observers)
    thick = thickness_weight.reshape(n_obs, n_panel, width, observers)
    piece = jax.ShapeDtypeStruct((2 * n_obs * width + EXTRA, observers), jnp.bfloat16)
    message, own, to_c, to_x, to_xc = pl.pallas_call(
        functools.partial(pack_kernel, n_panel, n_obs, cap),
        out_shape=[jax.ShapeDtypeStruct((rows + EXTRA, 2 * steps), jnp.bfloat16)] + [piece] * n_panel,
        in_specs=[hbm] * 5,
        out_specs=[vmem] * (1 + n_panel),
        scratch_shapes=[
            pltpu.VMEM((2 * rows, steps), jnp.bfloat16),
            pltpu.VMEM((1, rows), jnp.int32),
            pltpu.SMEM((1, nblocks), jnp.int32),
            pltpu.SemaphoreType.DMA((n_panel, 2)),
            pltpu.SemaphoreType.DMA((3,)),
        ],
        compiler_params=params,
    )(
        *(
            pltpu.with_memory_space_constraint(value, pltpu.HBM)
            for value in (
                les_rows.reshape(2 * rows, steps),
                les_dest.reshape(1, rows),
                delays.reshape(1, nblocks),
                load,
                thick,
            )
        )
    )
    from_x, from_xc, from_c = along_panel(to_x, 2), along_panel(to_xc, 3), along_panel(to_c, 1)
    ranges = range(4, n_obs, 4)
    far = [along_obs(message, k) for k in ranges]
    later, from_c = lax.optimization_barrier((message, from_c))
    near = along_obs(later, 3)
    a = pl.pallas_call(
        join_kernel,
        out_shape=jax.ShapeDtypeStruct((n_obs // 4 * (rows + EXTRA), 2 * steps), jnp.bfloat16),
        in_specs=[vmem] * (n_obs // 4),
        out_specs=vmem,
        compiler_params=params,
        cost_estimate=pl.CostEstimate(flops=4*10**9, bytes_accessed=0, transcendentals=0),
    )(message, *far)
    ya, b = along_obs(a, 1), along_obs(a, 2)
    again, near = lax.optimization_barrier((jnp.concatenate(far, axis=0), near))
    yb = jnp.concatenate([near, along_obs(again, 3)], axis=0)

    buffers, pieces = (a, ya, b, yb), (own, from_c, from_x, from_xc)
    late = pl.pallas_call(
        late_kernel,
        out_shape=jax.ShapeDtypeStruct((8 * (n_panel - 2), observers), jnp.int32),
        in_specs=[vmem] * (n_panel - 2),
        out_specs=vmem,
        compiler_params=params,
        cost_estimate=pl.CostEstimate(flops=2*10**9, bytes_accessed=0, transcendentals=0),
    )(*pieces[2:])
    share = jax.ShapeDtypeStruct((steps // n_panel, observers), jnp.float32)
    shares = pl.pallas_call(
        functools.partial(part_kernel, n_panel, n_obs, cap),
        out_shape=[share] * n_panel,
        in_specs=[vmem] * (5 + n_panel),
        out_specs=[vmem] * n_panel,
        scratch_shapes=[pltpu.VMEM((2 * steps, observers), jnp.float32)],
        compiler_params=params,
        cost_estimate=pl.CostEstimate(flops=1, bytes_accessed=0, transcendentals=0),
    )(*buffers, *pieces, late)
    total = shares[0]
    for k in (2, 3, 1):
        total = total + along_panel(shares[k], k)
    return total


def solution(mesh):
    placed = (
        P(("panel", "obs"), None, None),
        P(("panel", "obs"), None),
        P("panel", "obs"),
        P("panel", "obs"),
        P("panel", "obs"),
    )
    return jax.shard_map(
        per_device, mesh=mesh, in_specs=placed, out_specs=P("panel", "obs"), check_vma=False
    )
```

```python
import functools

import jax
import jax.numpy as jnp
from jax import lax
from jax.experimental import pallas as pl
from jax.experimental.pallas import tpu as pltpu
from jax.sharding import PartitionSpec as P

PBLK = 512
FAR = (2, 3)
EXTRA = 16
VMEM_LIMIT = 48 * 1024 * 1024


def dot(a, b):
    return lax.dot_general(a, b, (((1,), (0,)), ((), ())), preferred_element_type=jnp.float32)


def pack_kernel(n_panel, n_obs, cap, rows_ref, dest_ref, delay_ref, load_ref, thick_ref, *refs):
    message_ref, chip_ref, *pieces = refs[:4]
    rows_in, dest_in, delay_in, sems, few = refs[4:]
    count = n_panel * n_obs
    me_p = lax.axis_index("panel")
    width = n_obs * cap
    depth = n_obs * width
    small = [
        pltpu.make_async_copy(src, dst, few.at[i])
        for i, (src, dst) in enumerate(((rows_ref, rows_in), (dest_ref, dest_in), (delay_ref, delay_in)))
    ]
    for copy in small:
        copy.start()
    copies = []
    for at, k in enumerate(FAR):
        for i, ref in enumerate((load_ref, thick_ref)):
            there = pieces[at].at[pl.ds(i * depth, depth)].reshape(n_obs, width, ref.shape[3])
            copies.append(pltpu.make_async_copy(ref.at[:, me_p ^ k], there, sems.at[at, i]))
            copies[-1].start()
    for i, ref in enumerate((load_ref, thick_ref)):
        there = chip_ref.at[pl.ds(2 * i * depth, 2 * depth)].reshape(n_obs, 2, width, ref.shape[3])
        copies.append(pltpu.make_async_copy(ref.at[:, pl.ds(me_p // 2 * 2, 2)], there, sems.at[2, i]))
        copies[-1].start()
    rows, steps = rows_ref.shape[0] // 2, rows_ref.shape[1]
    nblocks = delay_ref.shape[1]
    for copy in small:
        copy.wait()
    lane = lax.broadcasted_iota(jnp.int32, (EXTRA, load_ref.shape[3]), 1)
    late = jnp.zeros(lane.shape, jnp.int32)
    for b in range(nblocks):
        late = jnp.where(lane == b, delay_in[0, b], late)
    for ref in (chip_ref, *pieces):
        ref[ref.shape[0] - EXTRA :, :] = late.astype(jnp.float32).astype(jnp.bfloat16)
    r0 = lax.broadcasted_iota(jnp.int32, (rows, 2 * rows), 0)
    r1 = lax.broadcasted_iota(jnp.int32, (rows, 2 * rows), 1)
    value = rows_in[...]
    pressure = dot((r1 == 2 * r0).astype(jnp.bfloat16), value).astype(jnp.bfloat16)
    velocity = dot((r1 == 2 * r0 + 1).astype(jnp.bfloat16), value).astype(jnp.bfloat16)
    t0 = lax.broadcasted_iota(jnp.int32, (steps, steps), 0)
    t1 = lax.broadcasted_iota(jnp.int32, (steps, steps), 1)
    slope = jnp.where(t0 == t1 + 1, 0.5, jnp.where(t0 == t1 - 1, -0.5, 0.0)).astype(jnp.bfloat16)
    message_ref[0:rows, 0:steps] = pressure
    message_ref[0:rows, steps:] = dot(velocity, slope).astype(jnp.bfloat16)
    dest = dest_in[...]
    onehot = lax.broadcasted_iota(jnp.int32, (count, rows), 0) == dest
    q0 = lax.broadcasted_iota(jnp.int32, (rows, rows), 0)
    q1 = lax.broadcasted_iota(jnp.int32, (rows, rows), 1)
    before = dot(onehot.astype(jnp.bfloat16), (q0 < q1).astype(jnp.bfloat16))
    rank = jnp.sum(jnp.where(onehot, before, 0.0), axis=0, keepdims=True)
    tail = jnp.zeros((EXTRA, steps), jnp.float32)
    message_ref[rows:, 0:steps] = (tail + dest.astype(jnp.float32)).astype(jnp.bfloat16)
    message_ref[rows:, steps:] = (tail + rank).astype(jnp.bfloat16)
    for copy in copies:
        copy.wait()


def late_kernel(*refs):
    for i, ref in enumerate(refs[:-1]):
        tail = ref[ref.shape[0] - EXTRA :, :].astype(jnp.float32)[0:8]
        refs[-1][8 * i : 8 * i + 8] = tail.astype(jnp.int32)


def join_kernel(*refs):
    at = 0
    for ref in refs[:-1]:
        refs[-1][at : at + ref.shape[0]] = ref[...]
        at += ref.shape[0]


def part_kernel(n_panel, n_obs, cap, *refs):
    buffers, pieces, late_ref = refs[:4], refs[4 : 4 + n_panel], refs[4 + n_panel]
    outs, acc_ref = refs[5 + n_panel : -1], refs[-1]
    count = n_panel * n_obs
    me_p = lax.axis_index("panel")
    me_o = lax.axis_index("obs")
    rows = refs[0].shape[0] // (n_obs // 4) - EXTRA
    steps = refs[0].shape[1] // 2
    per = 16 // cap
    width = n_obs * cap
    depth = n_obs * width
    acc_ref[...] = jnp.zeros_like(acc_ref)
    slot_ids = lax.broadcasted_iota(jnp.int32, (count * 16, per * rows), 0)
    groups, starts = [], []
    for quad in range(n_obs // per):
        values, places = [], []
        for i in range(per):
            j = quad * per + i
            ref, base = buffers[j % 4], (j // 4) * (rows + EXTRA)
            tail = ref[base + rows : base + rows + EXTRA, :].astype(jnp.float32)[0:1].astype(jnp.int32)
            dest, rank = tail[:, 0:rows], tail[:, steps : steps + rows]
            within = ((me_o % per) ^ i) * cap + rank
            places.append((dest ^ (me_p * n_obs)) * 16 + within)
            values.append(ref[base : base + rows, :])
        pick = (slot_ids == jnp.concatenate(places, axis=1)).astype(jnp.bfloat16)
        groups.append(dot(pick, jnp.concatenate(values, axis=0)).astype(jnp.bfloat16))
        starts.append(((me_o // per) ^ quad) * 16)
    for k in range(n_panel):
        delays = late_ref[8 * k : 8 * k + 8][0:1]
        scale, shift = (2, me_p % 2 * width) if k < 2 else (1, 0)
        for b in range(n_obs // 2):
            row = 32 * (k * (n_obs // 2) + b)
            source = jnp.concatenate(
                [g[row : row + 32, c * steps : (c + 1) * steps] for c in range(2) for g in groups], axis=0
            )
            weights = jnp.concatenate(
                [
                    pieces[k][pl.ds(pl.multiple_of(scale * (c * depth + (2 * b + h) * width) + shift + start, 16), 16), :]
                    for c in range(2)
                    for start in starts
                    for h in range(2)
                ],
                axis=0,
            )
            acc_ref[pl.ds(delays[0, b], steps), :] += dot(source.T, weights)
    share = steps // n_panel
    for k in range(n_panel):
        start = pl.multiple_of((me_p ^ k) * share, share)
        outs[k][...] = acc_ref[pl.ds(start, share), :]


def per_device(les_rows, les_dest, loading_weight, thickness_weight, delays):
    n_panel = lax.axis_size("panel")
    n_obs = lax.axis_size("obs")
    count = n_panel * n_obs
    rows, _, steps = les_rows.shape
    cap = 2 * rows // count
    observers = loading_weight.shape[1]
    width = n_obs * cap
    nblocks = n_obs // 2
    params = pltpu.CompilerParams(vmem_limit_bytes=VMEM_LIMIT)
    vmem = pl.BlockSpec(memory_space=pltpu.VMEM)
    hbm = pl.BlockSpec(memory_space=pltpu.HBM)

    def along_panel(value, k):
        return lax.ppermute(value, "panel", [(i, i ^ k) for i in range(n_panel)])

    def along_obs(value, k):
        return lax.ppermute(value, "obs", [(i, i ^ k) for i in range(n_obs)])

    load = loading_weight.reshape(n_obs, n_panel, width, observers)
    thick = thickness_weight.reshape(n_obs, n_panel, width, observers)
    piece = jax.ShapeDtypeStruct((2 * n_obs * width + EXTRA, observers), jnp.bfloat16)
    chip = jax.ShapeDtypeStruct((4 * n_obs * width + EXTRA, observers), jnp.bfloat16)
    message, own, to_x, to_xc = pl.pallas_call(
        functools.partial(pack_kernel, n_panel, n_obs, cap),
        out_shape=[jax.ShapeDtypeStruct((rows + EXTRA, 2 * steps), jnp.bfloat16)] + [chip, piece, piece],
        in_specs=[hbm] * 5,
        out_specs=[vmem] * 4,
        scratch_shapes=[
            pltpu.VMEM((2 * rows, steps), jnp.bfloat16),
            pltpu.VMEM((1, rows), jnp.int32),
            pltpu.SMEM((1, nblocks), jnp.int32),
            pltpu.SemaphoreType.DMA((n_panel, 2)),
            pltpu.SemaphoreType.DMA((3,)),
        ],
        compiler_params=params,
    )(
        *(
            pltpu.with_memory_space_constraint(value, pltpu.HBM)
            for value in (
                les_rows.reshape(2 * rows, steps),
                les_dest.reshape(1, rows),
                delays.reshape(1, nblocks),
                load,
                thick,
            )
        )
    )
    from_x, from_xc, from_c = along_panel(to_x, 2), along_panel(to_xc, 3), along_panel(own, 1)
    ranges = range(4, n_obs, 4)
    far = [along_obs(message, k) for k in ranges]
    later, from_c = lax.optimization_barrier((message, from_c))
    near = along_obs(later, 3)
    a = pl.pallas_call(
        join_kernel,
        out_shape=jax.ShapeDtypeStruct((n_obs // 4 * (rows + EXTRA), 2 * steps), jnp.bfloat16),
        in_specs=[vmem] * (n_obs // 4),
        out_specs=vmem,
        compiler_params=params,
        cost_estimate=pl.CostEstimate(flops=4*10**9, bytes_accessed=0, transcendentals=0),
    )(message, *far)
    ya, b = along_obs(a, 1), along_obs(a, 2)
    again, near = lax.optimization_barrier((jnp.concatenate(far, axis=0), near))
    yb = jnp.concatenate([near, along_obs(again, 3)], axis=0)

    buffers, pieces = (a, ya, b, yb), (own, from_c, from_x, from_xc)
    late = pl.pallas_call(
        late_kernel,
        out_shape=jax.ShapeDtypeStruct((8 * n_panel, observers), jnp.int32),
        in_specs=[vmem] * n_panel,
        out_specs=vmem,
        compiler_params=params,
        cost_estimate=pl.CostEstimate(flops=2*10**9, bytes_accessed=0, transcendentals=0),
    )(*pieces)
    share = jax.ShapeDtypeStruct((steps // n_panel, observers), jnp.float32)
    shares = pl.pallas_call(
        functools.partial(part_kernel, n_panel, n_obs, cap),
        out_shape=[share] * n_panel,
        in_specs=[vmem] * (5 + n_panel),
        out_specs=[vmem] * n_panel,
        scratch_shapes=[pltpu.VMEM((2 * steps, observers), jnp.float32)],
        compiler_params=params,
        cost_estimate=pl.CostEstimate(flops=1, bytes_accessed=0, transcendentals=0),
    )(*buffers, *pieces, late)
    total = shares[0]
    for k in (3, 1, 2):
        total = total + along_panel(shares[k], k)
    return total


def solution(mesh):
    placed = (
        P(("panel", "obs"), None, None),
        P(("panel", "obs"), None),
        P("panel", "obs"),
        P("panel", "obs"),
        P("panel", "obs"),
    )
    return jax.shard_map(
        per_device, mesh=mesh, in_specs=placed, out_specs=P("panel", "obs"), check_vma=False
    )
```
